1024 devices in a mesh: ex: 64 (over y, x), ey: 16 (over z, core).
Axes of the slice: x: 8, y: 8, z: 8, core: 2. Of those that a mesh axis runs over, the one named last changes fastest.
Arguments:
- dyn_field: float32 [72, 512, 2048], P(None, 'ex', 'ey'), may hold values from -6 to 6
- crm_state: float32 [32768, 58, 128], P(('ex', 'ey')), may hold values from -6 to 6
- subcycles: int32 [32768], P(('ex', 'ey')), may hold values from 1 to 12, as said below
- dest_slot: int32 [32768], P(('ex', 'ey')), may hold values from -1 to 31, as said below
Outputs:
- dyn_out: float32 [72, 512, 2048], P(None, 'ex', 'ey')
- crm_out: float32 [32768, 58, 128], P(('ex', 'ey'))
The draws below stay inside these ranges and needn't reach their ends.
Inputs may be any that keep to these rules, and one draw needn't show every extreme that they name: `subcycles`: some block of each draw has 12 substeps. Within each ey row the subset's blocks, in order of device and block index, are dealt to the row's owners in turn: the r-th goes to owner r modulo the ey axis's length, and dest_slot = owner * 2 + (its index among its device's subset blocks) divided by the ey axis's length, rounded down. Every owner receives exactly 16 blocks, and some device of each row has all 32 of its blocks in the subset.
All inputs are finite; a program needn't handle non-finite values.
Results may differ from the reference program's by a relative error of at most 0.0003.
Values sent between devices are 32-bit elements; how exact they have to be, the bound alone decides.
A program may use at most 32 MiB of HBM per device.

```python
import jax
import jax.numpy as jnp
from jax import lax

GLEV = 72
LEV = 58
COLS = 64
CX = 8
CY = 128
B_DEV = 32
DSTEPS = 3
MAXSUB = 12
CAP = 2
BLOCKS = 32768
NX = 512
NY = 2048
N_EX = 64
N_EY = 16


def plan_blocks(key):
    rows_key, pair_key, perm_key, count_key, heavy_key = jax.random.split(key, 5)
    half = B_DEV // 2
    shifts = jax.random.randint(pair_key, (N_EX, N_EY // 2), 0, half + 1).astype(jnp.int32)
    shifts = shifts.at[:, 0].set(half)
    orders = jax.vmap(lambda sub: jax.random.permutation(sub, N_EY))(jax.random.split(rows_key, N_EX)).astype(jnp.int32)
    values = jnp.stack([half + shifts, half - shifts], axis=2).reshape(N_EX, N_EY)
    live_count = jnp.zeros((N_EX, N_EY), jnp.int32).at[jnp.arange(N_EX, dtype=jnp.int32)[:, None], orders].set(values)
    within = jax.vmap(lambda sub: jax.random.permutation(sub, B_DEV))(jax.random.split(perm_key, N_EX * N_EY)).astype(jnp.int32)
    within = within.reshape(N_EX, N_EY, B_DEV)
    live = within < live_count[:, :, None]
    inner = jnp.cumsum(live.astype(jnp.int32), axis=2) - 1
    offset = jnp.cumsum(live_count, axis=1) - live_count
    ranking = offset[:, :, None] + inner
    owner = ranking % N_EY
    placed = inner // N_EY
    slots = jnp.where(live, owner * CAP + placed, -1).astype(jnp.int32)
    counts = jax.random.randint(count_key, (N_EX, N_EY, B_DEV), 1, MAXSUB // 2 + 1).astype(jnp.int32)
    heavy = jax.random.randint(heavy_key, (N_EX, N_EY, B_DEV), 0, 8) == 0
    counts = jnp.where(heavy, MAXSUB, counts)
    counts = jnp.where(live & (ranking == 0), MAXSUB, counts).astype(jnp.int32)
    return (slots.reshape(-1), counts.reshape(-1))


def draw_subcycles(key, part):
    return plan_blocks(key)[1]


def draw_dest_slot(key, part):
    return plan_blocks(key)[0]


def steps_of(own_key, shape, cuts, smallest, top_value):
    loudness = 1.0
    for axis_at, parts in cuts:
        draws = jax.random.uniform(jax.random.fold_in(jax.random.fold_in(own_key, 6), axis_at), (parts,), jnp.float32, smallest / len(cuts), top_value / len(cuts))
        loudness = loudness * jnp.repeat(jnp.exp(draws), shape[axis_at] // parts).reshape((-1,) + (1,) * (len(shape) - 1 - axis_at))
    return loudness


def noise(rng, extent, spread, limit, cuts=(), kind=jnp.bfloat16):
    entries = jax.random.normal(rng, extent, jnp.float32) * spread
    if len(cuts) > 0:
        entries = steps_of(rng, extent, cuts, -0.22, 0.18) * entries
    return jnp.clip(entries, min=-limit, max=limit).astype(kind)


def setup_inputs(seed: int = 0) -> dict:
    keys = jax.random.split(jax.random.key(seed), 5)
    dyn_field = noise(keys[0], (GLEV, NX, NY), 1.0, 6.0, ((1, 64), (2, 16)), jnp.float32)
    crm_state = noise(keys[1], (BLOCKS, LEV, 2 * COLS), 1.0, 6.0, ((0, 1024),), jnp.float32)
    subcycles = draw_subcycles(jax.random.fold_in(keys[4], 71), 0)
    dest_slot = draw_dest_slot(jax.random.fold_in(keys[4], 71), 0)
    return dict(dyn_field=dyn_field, crm_state=crm_state, subcycles=subcycles, dest_slot=dest_slot)


mixing = 0.2
damping_coefficient = 0.1
phase_change_warming = 0.5
droplet_formation_speed = 0.5
dewpoint_reference_humidity = 0.5
dewpoint_slope = 0.3
spread_rate = 0.2


def cloud_update(fields, coarse_cell_sounding, counts, bound):
    tile_clusters = fields.shape[0]
    altitude_layers = fields.shape[1]
    stack_sequence = fields.shape[2] // 2

    def substep(counter, current):
        bisected_pieces = current.reshape(tile_clusters, altitude_layers, 2, stack_sequence)
        across = jnp.roll(bisected_pieces, 1, axis=3) + jnp.roll(bisected_pieces, -1, axis=3) - 2.0 * bisected_pieces
        padded = jnp.pad(bisected_pieces, ((0, 0), (1, 1), (0, 0), (0, 0)))
        upward = padded[:, 2:] + padded[:, :-2] - 2.0 * bisected_pieces
        turbulent_diffusion_contribution = mixing * (across + upward)
        ambient_warmth = bisected_pieces[:, :, 0]
        specific_humidity = bisected_pieces[:, :, 1]
        excess_humidity = droplet_formation_speed * jnp.maximum(specific_humidity - dewpoint_reference_humidity * jnp.exp(dewpoint_slope * ambient_warmth), 0.0)
        pullback_intensity = damping_coefficient * (coarse_cell_sounding - jnp.mean(ambient_warmth, axis=-1))
        upcoming_warmth = ambient_warmth + turbulent_diffusion_contribution[:, :, 0] + pullback_intensity[:, :, None] + phase_change_warming * excess_humidity
        upcoming_humidity = specific_humidity + turbulent_diffusion_contribution[:, :, 1] - excess_humidity
        updated_condition = jnp.stack([upcoming_warmth, upcoming_humidity], axis=2).reshape(tile_clusters, altitude_layers, 2 * stack_sequence)
        return jnp.where((counter < counts)[:, None, None], updated_condition, current)

    finished = lax.fori_loop(0, bound, substep, fields)
    tendency = jnp.mean(finished[:, :, :stack_sequence] - fields[:, :, :stack_sequence], axis=-1)
    return finished, tendency


def diffuse(field):
    near = jnp.roll(field, 1, 1) + jnp.roll(field, -1, 1) + jnp.roll(field, 1, 2) + jnp.roll(field, -1, 2)
    return field + spread_rate * (near - 4.0 * field)


def reference(dyn_field, crm_state, subcycles, dest_slot):
    field = dyn_field
    for repeat in range(DSTEPS):
        field = diffuse(field)
    every_block = jnp.arange(BLOCKS, dtype=jnp.int32)
    device = every_block // B_DEV
    column = (every_block % B_DEV) * (CX * CY // B_DEV)
    row_x = (device // N_EY) * CX + column // CY
    row_y = (device % N_EY) * CY + column % CY
    coarse_cell_sounding = dyn_field[:LEV, row_x, row_y].T
    active = jnp.where(dest_slot >= 0, subcycles, 0).astype(jnp.int32)
    grouped = N_EY * B_DEV

    def per_row(inputs):
        return cloud_update(inputs[0], inputs[1], inputs[2], MAXSUB)

    finished, tendency = lax.map(per_row, (crm_state.reshape(N_EX, grouped, LEV, 2 * COLS), coarse_cell_sounding.reshape(N_EX, grouped, LEV), active.reshape(N_EX, grouped)))
    crm_out = finished.reshape(BLOCKS, LEV, 2 * COLS)
    tendency = tendency.reshape(BLOCKS, LEV)
    dyn_out = field.at[:LEV, row_x, row_y].add(tendency.T)
    return dyn_out, crm_out
```

```python
import functools

import jax
import jax.numpy as jnp
import ml_dtypes
import numpy as np
from jax import lax
from jax.experimental import pallas as pl
from jax.experimental.pallas import tpu as pltpu
from jax.sharding import PartitionSpec as P

F32 = jnp.float32
BF16 = jnp.bfloat16
MESH = pl.DeviceIdType.MESH

GLEV, LEV, COLS, CX, CY, B_DEV, MAXSUB = 72, 58, 64, 8, 128, 32, 12
PAIRS = B_DEV // 2
ROWS = 64
PAD = 8
GROUP = 4
HALO = 3
PACK = 16
PACKS = (GLEV + PACK - 1) // PACK
CHUNKS = 4
RATE = 0.3 * float(np.log2(np.e))
SCALED_T = RATE
SCALED_Q = 2.0


def tables():
    lane = np.arange(128)
    half, col = lane // COLS, lane % COLS
    same = half[:, None] == half[None, :]
    gap = (col[:, None] - col[None, :]) % COLS
    near = same & ((gap == 0) | (gap == 1) | (gap == COLS - 1))
    moist = near.astype(np.float32)
    warm = moist - same.astype(np.float32) / 128.0
    step = np.stack([np.concatenate([m, m]) for m in (warm, moist)])
    pick = np.zeros((128, 256), np.float32)
    pick[32 * (np.arange(256) // COLS), np.arange(256)] = 1.0
    pick = np.concatenate([pick, pick])
    mean = np.zeros((2, 128, 128), np.float32)
    for pair in range(2):
        mean[pair, lane, 32 * (2 * pair + half)] = 1.0 / COLS
    mean = np.concatenate([mean[0], mean[0], mean[1], mean[1]])
    return [t.astype(ml_dtypes.bfloat16) for t in (step, pick, mean)]


def halves(x):
    high = x.astype(BF16)
    low = (x - high.astype(F32)).astype(BF16)
    return jnp.concatenate([high, low], axis=1)


def dot(x, m):
    return jnp.dot(x, m, preferred_element_type=F32)


def kernel(
    sizes, sub_ref, slot_ref, dyn_hbm, crm_hbm, step_ref, pick_ref, mean_ref,
    dyn_out_hbm, crm_out_hbm,
    field, crm, crm_new, temp, moist, first, pull, count,
    tall, send_rows, recv_rows, send_cols, recv_cols, edge, tend, result,
    in_sem, field_sem, out_sem, result_sem, send_sem, recv_sem,
):
    nex, ney = sizes
    ex, ey = lax.axis_index("ex"), lax.axis_index("ey")
    around = [(dx, dy) for dx in (-1, 0, 1) for dy in (-1, 0, 1) if (dx, dy) != (0, 0)]

    def device(dx, dy):
        return (lax.rem(ex + dx + nex, nex), lax.rem(ey + dy + ney, ney))

    barrier = pltpu.get_barrier_semaphore()
    for at in around:
        pl.semaphore_signal(barrier, inc=1, device_id=device(*at), device_id_type=MESH)

    load_field = pltpu.make_async_copy(dyn_hbm, field, field_sem)
    load_field.start()
    per = B_DEV // CHUNKS
    loads = []
    for c in range(CHUNKS):
        part = pl.ds(c * per, per)
        loads.append(pltpu.make_async_copy(crm_hbm.at[part], crm.at[part], in_sem.at[c]))
        loads[-1].start()

    lane8 = lax.broadcasted_iota(jnp.int32, (8, 128), 1)
    left8 = lane8 < COLS
    for p in range(PAIRS):
        both = []
        for b in (2 * p, 2 * p + 1):
            both.append(jnp.where(slot_ref[b] >= 0, sub_ref[b], 0))
        count[p] = jnp.where(left8, both[0], both[1])
    zero = jnp.zeros((8, 128), F32)
    for buf in (temp, moist):
        for side in range(2):
            buf[side, 0:PAD, :] = zero
            buf[side, PAD + PAIRS * ROWS : PAD + PAIRS * ROWS + PAD, :] = zero
            for p in range(PAIRS):
                buf[side, PAD + p * ROWS + ROWS - 8 : PAD + p * ROWS + ROWS, :] = zero

    load_field.wait()
    for r in range(HALO):
        send_rows[0, r] = field[pl.ds(r, GLEV, stride=CX), :]
        send_rows[1, r] = field[pl.ds(CX - HALO + r, GLEV, stride=CX), :]
    for g in range(PACKS):
        head = zero
        tail = zero
        for i in range(min(PACK, GLEV - g * PACK)):
            tile = field[pl.ds((g * PACK + i) * CX, CX), :]
            tile = pltpu.roll(tile, 8 * i, 1) if i else tile
            head = jnp.where(lane8 // 8 == i, tile, head)
            tail = jnp.where(lane8 // 8 == (i - 1) % PACK, tile, tail)
        send_cols[0, g] = head
        send_cols[1, g] = tail

    pl.semaphore_wait(barrier, len(around))
    copies = []
    for k, (dx, dy) in enumerate(around):
        if dy == 0:
            src, dst = send_rows.at[(dx + 1) // 2], recv_rows.at[(1 - dx) // 2]
        else:
            src, dst = send_cols.at[(dy + 1) // 2], recv_cols.at[1 - dx, (1 - dy) // 2]
        copies.append(
            pltpu.make_async_remote_copy(
                src_ref=src,
                dst_ref=dst,
                send_sem=send_sem.at[k],
                recv_sem=recv_sem.at[k],
                device_id=device(dx, dy),
                device_id_type=MESH,
            )
        )
        copies[-1].start()

    for r in range(CX):
        host = field[pl.ds(r, ROWS, stride=CX), :]
        wide = (0.1 * SCALED_T) * dot(halves(host), pick_ref[...])
        for s in range(2):
            pull[pl.ds((2 * r + s) * ROWS, ROWS), :] = wide[:, 128 * s : 128 * s + 128]

    left = lax.broadcasted_iota(jnp.int32, (LEV, 128), 1) < COLS
    for c in range(CHUNKS):
        loads[c].wait()
        for p in range(c * per // 2, (c + 1) * per // 2):
            one, two = crm[2 * p], crm[2 * p + 1]
            t = SCALED_T * jnp.where(left, one, pltpu.roll(two, COLS, 1))
            q = SCALED_Q * jnp.where(left, pltpu.roll(one, COLS, 1), two)
            temp[0, pl.ds(PAD + p * ROWS, LEV), :] = t
            moist[0, pl.ds(PAD + p * ROWS, LEV), :] = q

    real = lax.broadcasted_iota(jnp.int32, (8, 128), 0) < LEV - (ROWS - 8)

    def substep(n, old, new):
        for g in range(PAIRS // GROUP):
            base, rows = PAD + g * GROUP * ROWS, GROUP * ROWS
            here = pl.ds(base, rows)
            t, q = temp[old, here, :], moist[old, here, :]
            mt = dot(halves(t), step_ref[0])
            mq = dot(halves(q), step_ref[1])
            vt = temp[old, pl.ds(base - 1, rows), :] + temp[old, pl.ds(base + 1, rows), :]
            vq = moist[old, pl.ds(base - 1, rows), :] + moist[old, pl.ds(base + 1, rows), :]
            e = jnp.maximum(q - jnp.exp2(t), 0.0)
            t_new = 0.2 * (mt + vt) + (pull[pl.ds(g * rows, rows), :] + (0.125 * SCALED_T) * e)
            q_new = 0.2 * (mq + vq) - 0.5 * e
            masks = []
            for p in range(g * GROUP, (g + 1) * GROUP):
                on = n < count[p]
                masks += [on] * (ROWS // 8 - 1) + [on & real]
            on = jnp.concatenate(masks, axis=0)
            temp[new, here, :] = jnp.where(on, t_new, t)
            moist[new, here, :] = jnp.where(on, q_new, q)

    @pl.loop(0, MAXSUB // 2)
    def _(n):
        substep(2 * n, 0, 1)
        substep(2 * n + 1, 1, 0)

    outs = []
    for c in range(CHUNKS):
        for p in range(c * per // 2, (c + 1) * per // 2):
            t = (1.0 / SCALED_T) * temp[0, pl.ds(PAD + p * ROWS, LEV), :]
            q = (1.0 / SCALED_Q) * moist[0, pl.ds(PAD + p * ROWS, LEV), :]
            crm_new[2 * p] = jnp.where(left, t, pltpu.roll(q, COLS, 1))
            crm_new[2 * p + 1] = jnp.where(left, pltpu.roll(t, COLS, 1), q)
            first[p] = t - jnp.where(left, crm[2 * p], pltpu.roll(crm[2 * p + 1], COLS, 1))
        part = pl.ds(c * per, per)
        outs.append(pltpu.make_async_copy(crm_new.at[part], crm_out_hbm.at[part], out_sem.at[c]))
        outs[-1].start()
    for r in range(CX):
        change = jnp.concatenate([halves(first[2 * r]), halves(first[2 * r + 1])], axis=1)
        tend[pl.ds(r, LEV, stride=CX), :] = dot(change, mean_ref[...])

    for copy in copies:
        copy.wait()
    for r in range(HALO):
        tall[pl.ds(8 - HALO + r, GLEV, stride=24), :] = recv_rows[0, r]
        tall[pl.ds(16 + r, GLEV, stride=24), :] = recv_rows[1, r]
    for level in range(GLEV):
        tall[pl.ds(level * 24 + 8, CX), :] = field[pl.ds(level * CX, CX), :]
    low_lanes = lane8 % 8 < 4
    for g in range(PACKS):
        for at in range(3):
            edge[g, 8 * at : 8 * at + 8, :] = jnp.where(low_lanes, recv_cols[at, 1, g], recv_cols[at, 0, g])

    first_lane, last_lane = lane8 == 0, lane8 == 127

    def spread(c, e):
        cr, cl = pltpu.roll(c, 1, 1), pltpu.roll(c, 127, 1)
        er, el = pltpu.roll(e, 1, 1), pltpu.roll(e, 127, 1)
        c_new = c + (jnp.where(first_lane, er, cr) + jnp.where(last_lane, el, cl))
        e_new = e + (jnp.where(first_lane, cr, er) + jnp.where(last_lane, cl, el))
        return c_new, e_new

    def sums(rows):
        at = [rows(k) for k in range(-HALO, HALO + 1)]
        return at[3], at[2] + at[4], at[1] + at[5], at[0] + at[6]

    for g in range(PACKS):
        packed = sums(lambda k: edge[g, pl.ds(8 + k, 8), :])
        for i in range(min(PACK, GLEV - g * PACK)):
            level = g * PACK + i
            own = pl.ds(level * CX, CX)
            e = [pltpu.roll(x, 128 - 8 * i, 1) if i else x for x in packed]
            c = sums(lambda k: tall[pl.ds(level * 24 + 8 + k, 8), :])
            x, y = spread(c[0], e[0])
            x, y = spread(x + 3.0 * c[1], y + 3.0 * e[1])
            x, y = spread(x + (6.0 * c[0] + 3.0 * c[2]), y + (6.0 * e[0] + 3.0 * e[2]))
            done = 0.008 * (x + (3.0 * c[1] + c[3]))
            result[own, :] = done + tend[own, :] if level < LEV else done
    store = pltpu.make_async_copy(result, dyn_out_hbm, result_sem)
    store.start()
    for out in outs:
        out.wait()
    store.wait()


def shards(sizes, dyn_field, crm_state, subcycles, dest_slot):
    any_space = pl.BlockSpec(memory_space=pl.ANY)
    smem = pl.BlockSpec(memory_space=pltpu.SMEM)
    vmem = pl.BlockSpec(memory_space=pltpu.VMEM)
    state = (2, 2 * PAD + PAIRS * ROWS, 128)
    dyn_out, crm_out = pl.pallas_call(
        functools.partial(kernel, sizes),
        out_shape=(
            jax.ShapeDtypeStruct((GLEV * CX, CY), F32),
            jax.ShapeDtypeStruct(crm_state.shape, F32),
        ),
        in_specs=[smem, smem, any_space, any_space, vmem, vmem, vmem],
        out_specs=(any_space, any_space),
        scratch_shapes=[
            pltpu.VMEM((GLEV * CX, CY), F32),
            pltpu.VMEM((B_DEV, LEV, 128), F32),
            pltpu.VMEM((B_DEV, LEV, 128), F32),
            pltpu.VMEM(state, F32),
            pltpu.VMEM(state, F32),
            pltpu.VMEM((PAIRS, LEV, 128), F32),
            pltpu.VMEM((PAIRS * ROWS, 128), F32),
            pltpu.VMEM((PAIRS, 8, 128), jnp.int32),
            pltpu.VMEM((GLEV * 24, CY), F32),
            pltpu.VMEM((2, HALO, GLEV, CY), F32),
            pltpu.VMEM((2, HALO, GLEV, CY), F32),
            pltpu.VMEM((2, PACKS, 8, 128), F32),
            pltpu.VMEM((3, 2, PACKS, 8, 128), F32),
            pltpu.VMEM((PACKS, 24, 128), F32),
            pltpu.VMEM((GLEV * CX, CY), F32),
            pltpu.VMEM((GLEV * CX, CY), F32),
            pltpu.SemaphoreType.DMA((CHUNKS,)),
            pltpu.SemaphoreType.DMA,
            pltpu.SemaphoreType.DMA((CHUNKS,)),
            pltpu.SemaphoreType.DMA,
            pltpu.SemaphoreType.DMA((8,)),
            pltpu.SemaphoreType.DMA((8,)),
        ],
        compiler_params=pltpu.CompilerParams(
            collective_id=0, has_side_effects=True, vmem_limit_bytes=48 * 1024 * 1024
        ),
    )(
        subcycles, dest_slot, dyn_field.reshape(GLEV * CX, CY), crm_state,
        *[jnp.asarray(t) for t in tables()],
    )
    return dyn_out.reshape(dyn_field.shape), crm_out


def solution(mesh):
    placed = (P(None, "ex", "ey"), P(("ex", "ey"), None, None), P(("ex", "ey")), P(("ex", "ey")))
    return jax.shard_map(
        functools.partial(shards, (mesh.shape["ex"], mesh.shape["ey"])),
        mesh=mesh,
        in_specs=placed,
        out_specs=(P(None, "ex", "ey"), P(("ex", "ey"), None, None)),
        check_vma=False,
    )
```

```python
import functools

import jax
import jax.numpy as jnp
import numpy as np
from jax import lax
from jax.experimental import pallas as pl
from jax.experimental.pallas import tpu as pltpu
from jax.sharding import PartitionSpec as P

F32 = jnp.float32
BF16 = jnp.bfloat16
MESH = pl.DeviceIdType.MESH

GLEV, LEV, COLS, CX, CY, B_DEV, MAXSUB = 72, 58, 64, 8, 128, 32, 12
PER_ROW = B_DEV // CX
STRIDE = CY // PER_ROW
ROWS = LEV * CX
GROWS = GLEV * CX
PAD = 8
SETS = PER_ROW // 2
CUTS = (0, 16, 30, 44, 58)
HALO = 3
PACK = 16
PACKS = (GLEV + PACK - 1) // PACK
GROUPS = GLEV // 8
CHUNKS = 2
VMEM_BYTES = 60 * 1024 * 1024
RATE = 0.3 * float(np.log2(np.e))
SCALED_T = RATE
SCALED_Q = 2.0
AROUND = [(1, 0), (1, -1), (1, 1), (0, -1), (0, 1), (-1, 0), (-1, -1), (-1, 1)]


def tables(step, pick, mean):
    def iotas(shape):
        return (lax.broadcasted_iota(jnp.int32, shape, d) for d in range(2))

    def where(flag, value):
        return jnp.where(flag, value, 0.0)

    row, col = iotas((256, 256))
    gap = (row - col) & (COLS - 1)
    same = row // COLS == col // COLS
    near = same & ((gap == 0) | (gap == 1) | (gap == COLS - 1))
    block = where(near, 1.0) - where(same & (row < 128), 1.0 / 128.0)
    step[0:256, :] = block.astype(BF16)
    step[256:512, :] = block.astype(BF16)
    block = where((row & 127) == STRIDE * (col // COLS), 1.0)
    pick[...] = block.astype(BF16)
    row, col = iotas((256, 128))
    for j in range(SETS):
        block = where(col == STRIDE * (2 * j + (row & 127) // COLS), 1.0 / COLS)
        mean[256 * j : 256 * j + 256, :] = block.astype(BF16)


def split(x):
    high = x.astype(BF16)
    return high, (x - high.astype(F32)).astype(BF16)


def dot(terms, m):
    return jnp.dot(jnp.concatenate(terms, axis=1), m, preferred_element_type=F32)


def kernel(
    sizes, sub_hbm, slot_hbm, dyn_hbm, crm_hbm,
    dyn_hbm_out, crm_hbm_out,
    result, crm_new, field, crm, sub, slot, step, pick, mean, temp, moist, pull,
    tall, send_rows, recv_rows, send_cols, recv_cols, send_far, recv_far, edge,
    load_sem, in_sem, out_sem, send_sem, recv_sem,
):
    nex, ney = sizes
    ex, ey = lax.axis_index("ex"), lax.axis_index("ey")

    def order(x, y):
        index = x * ney + y
        return jnp.where(index == 0, 6 * nex * ney + 5, 10 * index)

    def device(dx, dy):
        return lax.rem(ex + dx + nex, nex), lax.rem(ey + dy + ney, ney)

    mine = order(ex, ey)
    ahead = [order(*device(*at)) < mine for at in AROUND]
    n_ahead = sum(jnp.where(a, 1, 0) for a in ahead)

    barrier = pltpu.get_barrier_semaphore()
    for at, a in zip(AROUND, ahead):
        @pl.when(jnp.logical_not(a))
        def _():
            pl.semaphore_signal(barrier, inc=1, device_id=device(*at), device_id_type=MESH)

    small = [(dyn_hbm, field), (sub_hbm, sub), (slot_hbm, slot)]
    small = [pltpu.make_async_copy(src, dst, load_sem.at[i]) for i, (src, dst) in enumerate(small)]
    for copy in small:
        copy.start()
    loads = []
    per = LEV * B_DEV // CHUNKS
    for c in range(CHUNKS):
        part = pl.ds(c * per, per)
        loads.append(pltpu.make_async_copy(crm_hbm.at[part], crm.at[part], in_sem.at[c]))
        loads[-1].start()

    lane8 = lax.broadcasted_iota(jnp.int32, (8, 128), 1)
    row8 = lax.broadcasted_iota(jnp.int32, (8, 128), 0)
    left8 = lane8 < COLS
    zero = jnp.zeros((8, 128), F32)

    small[0].wait()
    for r in range(HALO):
        send_rows[1, r] = field[pl.ds(CX - 1 - r, GLEV, stride=CX), :]
    for r in range(HALO):
        send_rows[0, r] = field[pl.ds(r, GLEV, stride=CX), :]

    copies = []
    for k, (dx, dy) in enumerate(AROUND):
        side = (dy + 1) // 2
        if dy == 0:
            src, dst = send_rows.at[(dx + 1) // 2], recv_rows.at[(1 - dx) // 2]
        elif dx == 1:
            src, dst = send_far.at[side], recv_far.at[1 - side]
        else:
            src, dst = send_cols.at[side], recv_cols.at[-dx, 1 - side]
        copies.append(
            pltpu.make_async_remote_copy(
                src_ref=src,
                dst_ref=dst,
                send_sem=send_sem.at[k],
                recv_sem=recv_sem.at[k],
                device_id=device(dx, dy),
                device_id_type=MESH,
            )
        )

    def begin(k, flag):
        @pl.when(flag)
        def _():
            copies[k].start()

    @pl.when(n_ahead > 0)
    def _():
        pl.semaphore_wait(barrier, n_ahead)

    for k, (dx, dy) in enumerate(AROUND):
        if dy == 0:
            begin(k, ahead[k])

    for r in range(2):
        head, tail = zero, zero
        for g in range(GROUPS):
            tile = send_rows[1, r, 8 * g : 8 * g + 8, :]
            tile = pltpu.roll(tile, 8 * g, 1) if g else tile
            head = jnp.where(lane8 // 8 == g, tile, head)
            tail = jnp.where(lane8 // 8 == (g - 1) % 16, tile, tail)
        send_far[0, r] = head
        send_far[1, r] = tail
    for g in range(PACKS):
        head, tail = zero, zero
        for i in range(min(PACK, GLEV - g * PACK)):
            tile = field[pl.ds((g * PACK + i) * CX, CX), :]
            tile = pltpu.roll(tile, 8 * i, 1) if i else tile
            head = jnp.where(lane8 // 8 == i, tile, head)
            tail = jnp.where(lane8 // 8 == (i - 1) % PACK, tile, tail)
        send_cols[0, g] = head
        send_cols[1, g] = tail
    for k, (dx, dy) in enumerate(AROUND):
        if dy != 0:
            begin(k, ahead[k])

    small[1].wait()
    small[2].wait()
    active = jnp.where(slot[...] >= 0, sub[...], 0).astype(F32)
    lane32 = lax.broadcasted_iota(jnp.int32, (CX, B_DEV), 1)
    row32 = lax.broadcasted_iota(jnp.int32, (CX, B_DEV), 0)
    spread_out = jnp.broadcast_to(active, (CX, B_DEV))
    counts = []
    for k in range(PER_ROW):
        own = jnp.where(lane32 == PER_ROW * row32 + k, spread_out, 0.0)
        counts.append(jnp.sum(own, axis=1, keepdims=True))
    counts = [jnp.where(left8, counts[2 * j], counts[2 * j + 1]) for j in range(SETS)]

    for side in range(2):
        for j in range(SETS):
            for buf in (temp, moist):
                buf[side, j, 0:PAD, :] = zero
                buf[side, j, PAD + ROWS : PAD + ROWS + PAD, :] = zero

    tables(step, pick, mean)
    for a, b in zip(CUTS[:-1], CUTS[1:]):
        here = pl.ds(a * CX, (b - a) * CX)
        wide = (0.1 * SCALED_T) * dot(split(field[here, :]), pick[...])
        for j in range(SETS):
            pull[j, here, :] = wide[:, 128 * j : 128 * j + 128]

    def warm_and_moist(j, level):
        one, two = (crm[pl.ds(level * B_DEV + 2 * j + i, CX, stride=PER_ROW), :] for i in range(2))
        t = jnp.where(left8, one, pltpu.roll(two, COLS, 1))
        q = jnp.where(left8, pltpu.roll(one, COLS, 1), two)
        return t, q

    for load in loads:
        load.wait()
    for level in range(LEV):
        for j in range(SETS):
            t, q = warm_and_moist(j, level)
            temp[0, j, pl.ds(PAD + level * CX, CX), :] = SCALED_T * t
            moist[0, j, pl.ds(PAD + level * CX, CX), :] = SCALED_Q * q

    def substep(n, old, new):
        for j in range(SETS):
            on = n < counts[j]
            for a, b in zip(CUTS[:-1], CUTS[1:]):
                base, rows = PAD + a * CX, (b - a) * CX
                here, up, down = (pl.ds(base + s, rows) for s in (0, CX, -CX))
                t, q = temp[old, j, here, :], moist[old, j, here, :]
                (t1, t2), (q1, q2) = split(t), split(q)
                across = dot([t1, q1, t2, q2], step[...])
                vt = temp[old, j, up, :] + temp[old, j, down, :]
                vq = moist[old, j, up, :] + moist[old, j, down, :]
                e = jnp.maximum(q - jnp.exp2(t), 0.0)
                t_new = 0.2 * (across[:, :128] + vt) + (pull[j, pl.ds(a * CX, rows), :] + (0.125 * SCALED_T) * e)
                q_new = 0.2 * (across[:, 128:] + vq) - 0.5 * e
                mask = jnp.concatenate([on] * (b - a), axis=0)
                temp[new, j, here, :] = jnp.where(mask, t_new, t)
                moist[new, j, here, :] = jnp.where(mask, q_new, q)

    @pl.loop(0, MAXSUB // 2)
    def _(n):
        now = (2 * n).astype(F32)
        substep(now, 0, 1)
        substep(now + 1.0, 1, 0)

    outs = []
    for c in range(CHUNKS):
        for level in range(c * LEV // CHUNKS, (c + 1) * LEV // CHUNKS):
            for j in range(SETS):
                own = pl.ds(PAD + level * CX, CX)
                t = (1.0 / SCALED_T) * temp[0, j, own, :]
                q = (1.0 / SCALED_Q) * moist[0, j, own, :]
                temp[1, j, own, :] = t - warm_and_moist(j, level)[0]
                at = [pl.ds(level * B_DEV + 2 * j + i, CX, stride=PER_ROW) for i in range(2)]
                crm_new[at[0], :] = jnp.where(left8, t, pltpu.roll(q, COLS, 1))
                crm_new[at[1], :] = jnp.where(left8, pltpu.roll(t, COLS, 1), q)
        part = pl.ds(c * per, per)
        outs.append(pltpu.make_async_copy(crm_new.at[part], crm_hbm_out.at[part], out_sem.at[c]))
        outs[-1].start()

    def answer(dx):
        for k, at in enumerate(AROUND):
            if at[0] == dx:
                pair = AROUND.index((-at[0], -at[1]))
                copies[k].wait_recv()
                begin(pair, jnp.logical_not(ahead[pair]))

    answer(-1)
    answer(0)

    for level in range(GLEV):
        tall[pl.ds(level * 24, 8), :] = zero
        tall[pl.ds(level * 24 + 8, CX), :] = field[pl.ds(level * CX, CX), :]
    for r in range(HALO):
        tall[pl.ds(16 + r, GLEV, stride=24), :] = recv_rows[1, r]
    low_lanes = lane8 % 8 < 4
    for g in range(PACKS):
        edge[g, 0:8, :] = zero
        for at in range(2):
            edge[g, 8 * at + 8 : 8 * at + 16, :] = jnp.where(low_lanes, recv_cols[at, 1, g], recv_cols[at, 0, g])

    first_lane, last_lane = lane8 == 0, lane8 == 127

    def spread(c, e):
        cr, cl = pltpu.roll(c, 1, 1), pltpu.roll(c, 127, 1)
        er, el = pltpu.roll(e, 1, 1), pltpu.roll(e, 127, 1)
        c_new = c + (jnp.where(first_lane, er, cr) + jnp.where(last_lane, el, cl))
        e_new = e + (jnp.where(first_lane, cr, er) + jnp.where(last_lane, cl, el))
        return c_new, e_new

    def sums(rows):
        at = [rows(k) for k in range(-HALO, HALO + 1)]
        return at[3], at[2] + at[4], at[1] + at[5], at[0] + at[6]

    for g in range(PACKS):
        packed = sums(lambda k: edge[g, pl.ds(8 + k, 8), :])
        for i in range(min(PACK, GLEV - g * PACK)):
            level = g * PACK + i
            own = pl.ds(level * CX, CX)
            e = [pltpu.roll(x, 128 - 8 * i, 1) if i else x for x in packed]
            c = sums(lambda k: tall[pl.ds(level * 24 + 8 + k, 8), :])
            x, y = spread(c[0], e[0])
            x, y = spread(x + 3.0 * c[1], y + 3.0 * e[1])
            x, y = spread(x + (6.0 * c[0] + 3.0 * c[2]), y + (6.0 * e[0] + 3.0 * e[2]))
            result[own, :] = 0.008 * (x + (3.0 * c[1] + c[3]))
    for a, b in zip(CUTS[:-1], CUTS[1:]):
        here, padded = pl.ds(a * CX, (b - a) * CX), pl.ds(PAD + a * CX, (b - a) * CX)
        change = [part for j in range(SETS) for part in split(temp[1, j, padded, :])]
        result[here, :] += dot(change, mean[...])

    answer(1)
    far = [jnp.where(low_lanes, recv_far[1, r], recv_far[0, r]) for r in range(2)]
    for g in range(GROUPS):
        e1, e2 = (pltpu.roll(x, 128 - 8 * g, 1) if g else x for x in far)
        h1, h2, h3 = (recv_rows[0, r, 8 * g : 8 * g + 8, :] for r in range(HALO))
        u, v = spread(h1, e1)
        w, _ = spread(u + h2, v + e2)
        for r, add in enumerate((3.0 * (w + h1) + h3, 3.0 * u + h2, h1)):
            at = pl.ds(g * 8 * CX + r, 8, stride=CX)
            result[at, :] += 0.008 * add
    outs.append(pltpu.make_async_copy(result, dyn_hbm_out, out_sem.at[CHUNKS]))
    outs[-1].start()
    for copy in copies:
        copy.wait_send()
    for out in outs:
        out.wait()


def write(result, crm_new, dyn_out, crm_out, sems):
    parts = []
    for src, dst, n in ((crm_new, crm_out, 4), (result, dyn_out, 2)):
        rows = src.shape[0] // n
        for c in range(n):
            part = pl.ds(c * rows, rows)
            parts.append(pltpu.make_async_copy(src.at[part], dst.at[part], sems.at[len(parts)]))
    for part in parts:
        part.start()
    for part in parts:
        part.wait()


def shards(sizes, dyn_field, crm_state, subcycles, dest_slot):
    hbm = pl.BlockSpec(memory_space=pltpu.HBM)
    state = (2, SETS, ROWS + 2 * PAD, 128)
    dyn_shape = jax.ShapeDtypeStruct((GROWS, CY), F32)
    crm_shape = jax.ShapeDtypeStruct((LEV * B_DEV, 128), F32)
    result, crm_new = pl.pallas_call(
        functools.partial(kernel, sizes),
        out_shape=(dyn_shape, crm_shape),
        in_specs=[hbm] * 4,
        out_specs=(hbm, hbm),
        scratch_shapes=[
            pltpu.VMEM((GROWS, CY), F32),
            pltpu.VMEM((LEV * B_DEV, 128), F32),
            pltpu.VMEM((GROWS, CY), F32),
            pltpu.VMEM((LEV * B_DEV, 128), F32),
            pltpu.VMEM((1, B_DEV), jnp.int32),
            pltpu.VMEM((1, B_DEV), jnp.int32),
            pltpu.VMEM((512, 256), BF16),
            pltpu.VMEM((256, 256), BF16),
            pltpu.VMEM((512, 128), BF16),
            pltpu.VMEM(state, F32),
            pltpu.VMEM(state, F32),
            pltpu.VMEM((SETS, ROWS, 128), F32),
            pltpu.VMEM((GLEV * 24, CY), F32),
            pltpu.VMEM((2, HALO, GLEV, CY), F32),
            pltpu.VMEM((2, HALO, GLEV, CY), F32),
            pltpu.VMEM((2, PACKS, 8, 128), F32),
            pltpu.VMEM((2, 2, PACKS, 8, 128), F32),
            pltpu.VMEM((2, 2, 8, 128), F32),
            pltpu.VMEM((2, 2, 8, 128), F32),
            pltpu.VMEM((PACKS, 24, 128), F32),
            pltpu.SemaphoreType.DMA((3,)),
            pltpu.SemaphoreType.DMA((CHUNKS,)),
            pltpu.SemaphoreType.DMA((CHUNKS + 1,)),
            pltpu.SemaphoreType.DMA((8,)),
            pltpu.SemaphoreType.DMA((8,)),
        ],
        compiler_params=pltpu.CompilerParams(
            collective_id=0, has_side_effects=True, vmem_limit_bytes=VMEM_BYTES
        ),
    )(
        subcycles.reshape(1, B_DEV),
        dest_slot.reshape(1, B_DEV),
        dyn_field.reshape(GROWS, CY),
        jnp.transpose(crm_state, (1, 0, 2)).reshape(LEV * B_DEV, 128),
    )
    dyn_out, crm_out = pl.pallas_call(
        write,
        out_shape=(dyn_shape, crm_shape),
        in_specs=[hbm] * 2,
        out_specs=(hbm, hbm),
        scratch_shapes=[pltpu.SemaphoreType.DMA((6,))],
        compiler_params=pltpu.CompilerParams(vmem_limit_bytes=VMEM_BYTES),
    )(result, crm_new)
    crm_out = jnp.transpose(crm_out.reshape(LEV, B_DEV, 128), (1, 0, 2))
    return dyn_out.reshape(dyn_field.shape), crm_out


def solution(mesh):
    placed = (P(None, "ex", "ey"), P(("ex", "ey"), None, None), P(("ex", "ey")), P(("ex", "ey")))
    return jax.shard_map(
        functools.partial(shards, (mesh.shape["ex"], mesh.shape["ey"])),
        mesh=mesh,
        in_specs=placed,
        out_specs=(P(None, "ex", "ey"), P(("ex", "ey"), None, None)),
        check_vma=False,
    )
```

```python
import functools

import jax
import jax.numpy as jnp
import numpy as np
from jax import lax
from jax.experimental import pallas as pl
from jax.experimental.pallas import tpu as pltpu
from jax.sharding import PartitionSpec as P

F32 = jnp.float32
BF16 = jnp.bfloat16
MESH = pl.DeviceIdType.MESH

GLEV, LEV, COLS, CX, CY, B_DEV, MAXSUB = 72, 58, 64, 8, 128, 32, 12
PER_ROW = B_DEV // CX
STRIDE = CY // PER_ROW
ROWS = LEV * CX
GROWS = GLEV * CX
PAD = 8
SETS = PER_ROW // 2
CUTS = (0, 16, 30, 44, 58)
HALO = 3
PACK = 16
BATCH = 8
PACKS = (GLEV + PACK - 1) // PACK
GROUPS = GLEV // 8
CHUNKS = 2
VMEM_BYTES = 60 * 1024 * 1024
RATE = 0.3 * float(np.log2(np.e))
SCALED_T = RATE
SCALED_Q = 2.0
AROUND = [(1, 0), (1, -1), (1, 1), (0, -1), (0, 1), (-1, 0), (-1, -1), (-1, 1)]


def tables(step, pick, mean):
    def iotas(shape):
        return (lax.broadcasted_iota(jnp.int32, shape, d) for d in range(2))

    def where(flag, value):
        return jnp.where(flag, value, 0.0)

    row, col = iotas((256, 256))
    gap = (row - col) & (COLS - 1)
    same = row // COLS == col // COLS
    near = same & ((gap == 0) | (gap == 1) | (gap == COLS - 1))
    block = where(near, 1.0) - where(same & (row < 128), 1.0 / 128.0)
    step[0:256, :] = block.astype(BF16)
    step[256:512, :] = block.astype(BF16)
    block = where((row & 127) == STRIDE * (col // COLS), 1.0)
    pick[...] = block.astype(BF16)
    row, col = iotas((256, 128))
    for j in range(SETS):
        block = where(col == STRIDE * (2 * j + (row & 127) // COLS), 1.0 / COLS)
        mean[256 * j : 256 * j + 256, :] = block.astype(BF16)


def split(x):
    high = x.astype(BF16)
    return high, (x - high.astype(F32)).astype(BF16)


def dot(terms, m):
    return jnp.dot(jnp.concatenate(terms, axis=1), m, preferred_element_type=F32)


def kernel(
    sizes, sub_hbm, slot_hbm, dyn_hbm, crm_hbm,
    dyn_hbm_out, crm_hbm_out,
    result, crm_new, field, crm, sub, slot, step, pick, mean, temp, moist, pull,
    tall, send_rows, recv_rows, send_cols, recv_cols, send_far, recv_far, edge,
    load_sem, in_sem, out_sem, send_sem, recv_sem,
):
    nex, ney = sizes
    ex, ey = lax.axis_index("ex"), lax.axis_index("ey")

    def order(x, y):
        index = x * ney + y
        return jnp.where(index == 0, 6 * nex * ney + 5, 10 * index)

    def device(dx, dy):
        return lax.rem(ex + dx + nex, nex), lax.rem(ey + dy + ney, ney)

    mine = order(ex, ey)
    ahead = [order(*device(*at)) < mine for at in AROUND]
    n_ahead = sum(jnp.where(a, 1, 0) for a in ahead)

    barrier = pltpu.get_barrier_semaphore()
    for at, a in zip(AROUND, ahead):
        @pl.when(jnp.logical_not(a))
        def _():
            pl.semaphore_signal(barrier, inc=1, device_id=device(*at), device_id_type=MESH)

    small = [(dyn_hbm, field), (sub_hbm, sub), (slot_hbm, slot)]
    small = [pltpu.make_async_copy(src, dst, load_sem.at[i]) for i, (src, dst) in enumerate(small)]
    for copy in small:
        copy.start()
    loads = []
    per = LEV * B_DEV // CHUNKS
    for c in range(CHUNKS):
        part = pl.ds(c * per, per)
        loads.append(pltpu.make_async_copy(crm_hbm.at[part], crm.at[part], in_sem.at[c]))
        loads[-1].start()

    lane8 = lax.broadcasted_iota(jnp.int32, (8, 128), 1)
    row8 = lax.broadcasted_iota(jnp.int32, (8, 128), 0)
    left8 = lane8 < COLS
    zero = jnp.zeros((8, 128), F32)

    small[0].wait()
    for r in range(HALO):
        send_rows[1, r] = field[pl.ds(CX - 1 - r, GLEV, stride=CX), :]
    for r in range(HALO):
        send_rows[0, r] = field[pl.ds(r, GLEV, stride=CX), :]

    copies = []
    for k, (dx, dy) in enumerate(AROUND):
        side = (dy + 1) // 2
        if dy == 0:
            src, dst = send_rows.at[(dx + 1) // 2], recv_rows.at[(1 - dx) // 2]
        elif dx == 1:
            src, dst = send_far.at[side], recv_far.at[1 - side]
        else:
            src, dst = send_cols.at[side], recv_cols.at[-dx, 1 - side]
        copies.append(
            pltpu.make_async_remote_copy(
                src_ref=src,
                dst_ref=dst,
                send_sem=send_sem.at[k],
                recv_sem=recv_sem.at[k],
                device_id=device(dx, dy),
                device_id_type=MESH,
            )
        )

    def begin(k, flag):
        @pl.when(flag)
        def _():
            copies[k].start()

    @pl.when(n_ahead > 0)
    def _():
        pl.semaphore_wait(barrier, n_ahead)

    for k, (dx, dy) in enumerate(AROUND):
        if dy == 0:
            begin(k, ahead[k])

    for r in range(2):
        head, tail = zero, zero
        for g in range(GROUPS):
            tile = send_rows[1, r, 8 * g : 8 * g + 8, :]
            tile = pltpu.roll(tile, 8 * g, 1) if g else tile
            head = jnp.where(lane8 // 8 == g, tile, head)
            tail = jnp.where(lane8 // 8 == (g - 1) % 16, tile, tail)
        send_far[0, r] = head
        send_far[1, r] = tail
    for g in range(PACKS):
        head, tail = zero, zero
        for i in range(min(PACK, GLEV - g * PACK)):
            tile = field[pl.ds((g * PACK + i) * CX, CX), :]
            tile = pltpu.roll(tile, 8 * i, 1) if i else tile
            head = jnp.where(lane8 // 8 == i, tile, head)
            tail = jnp.where(lane8 // 8 == (i - 1) % PACK, tile, tail)
        send_cols[0, g] = head
        send_cols[1, g] = tail
    for k, (dx, dy) in enumerate(AROUND):
        if dy != 0:
            begin(k, ahead[k])

    small[1].wait()
    small[2].wait()
    active = jnp.where(slot[...] >= 0, sub[...], 0).astype(F32)
    lane32 = lax.broadcasted_iota(jnp.int32, (CX, B_DEV), 1)
    row32 = lax.broadcasted_iota(jnp.int32, (CX, B_DEV), 0)
    spread_out = jnp.broadcast_to(active, (CX, B_DEV))
    counts = []
    for k in range(PER_ROW):
        own = jnp.where(lane32 == PER_ROW * row32 + k, spread_out, 0.0)
        counts.append(jnp.sum(own, axis=1, keepdims=True))
    counts = [jnp.where(left8, counts[2 * j], counts[2 * j + 1]) for j in range(SETS)]

    for side in range(2):
        for j in range(SETS):
            for buf in (temp, moist):
                buf[side, j, 0:PAD, :] = zero
                buf[side, j, PAD + ROWS : PAD + ROWS + PAD, :] = zero

    tables(step, pick, mean)
    for a, b in zip(CUTS[:-1], CUTS[1:]):
        here = pl.ds(a * CX, (b - a) * CX)
        wide = (0.1 * SCALED_T) * dot(split(field[here, :]), pick[...])
        for j in range(SETS):
            pull[j, here, :] = wide[:, 128 * j : 128 * j + 128]

    def warm_and_moist(j, level):
        one, two = (crm[pl.ds(level * B_DEV + 2 * j + i, CX, stride=PER_ROW), :] for i in range(2))
        t = jnp.where(left8, one, pltpu.roll(two, COLS, 1))
        q = jnp.where(left8, pltpu.roll(one, COLS, 1), two)
        return t, q

    for load in loads:
        load.wait()
    for level in range(LEV):
        for j in range(SETS):
            t, q = warm_and_moist(j, level)
            temp[0, j, pl.ds(PAD + level * CX, CX), :] = SCALED_T * t
            moist[0, j, pl.ds(PAD + level * CX, CX), :] = SCALED_Q * q

    def substep(n, old, new):
        for j in range(SETS):
            on = n < counts[j]
            for a, b in zip(CUTS[:-1], CUTS[1:]):
                base, rows = PAD + a * CX, (b - a) * CX
                here, up, down = (pl.ds(base + s, rows) for s in (0, CX, -CX))
                t, q = temp[old, j, here, :], moist[old, j, here, :]
                (t1, t2), (q1, q2) = split(t), split(q)
                across = dot([t1, q1, t2, q2], step[...])
                vt = temp[old, j, up, :] + temp[old, j, down, :]
                vq = moist[old, j, up, :] + moist[old, j, down, :]
                e = jnp.maximum(q - jnp.exp2(t), 0.0)
                t_new = 0.2 * (across[:, :128] + vt) + (pull[j, pl.ds(a * CX, rows), :] + (0.125 * SCALED_T) * e)
                q_new = 0.2 * (across[:, 128:] + vq) - 0.5 * e
                mask = jnp.concatenate([on] * (b - a), axis=0)
                temp[new, j, here, :] = jnp.where(mask, t_new, t)
                moist[new, j, here, :] = jnp.where(mask, q_new, q)

    @pl.loop(0, MAXSUB // 2)
    def _(n):
        now = (2 * n).astype(F32)
        substep(now, 0, 1)
        substep(now + 1.0, 1, 0)

    outs = []
    for c in range(CHUNKS):
        for level in range(c * LEV // CHUNKS, (c + 1) * LEV // CHUNKS):
            for j in range(SETS):
                own = pl.ds(PAD + level * CX, CX)
                t = (1.0 / SCALED_T) * temp[0, j, own, :]
                q = (1.0 / SCALED_Q) * moist[0, j, own, :]
                temp[1, j, own, :] = t - warm_and_moist(j, level)[0]
                at = [pl.ds(level * B_DEV + 2 * j + i, CX, stride=PER_ROW) for i in range(2)]
                crm_new[at[0], :] = jnp.where(left8, t, pltpu.roll(q, COLS, 1))
                crm_new[at[1], :] = jnp.where(left8, pltpu.roll(t, COLS, 1), q)
        part = pl.ds(c * per, per)
        outs.append(pltpu.make_async_copy(crm_new.at[part], crm_hbm_out.at[part], out_sem.at[c]))
        outs[-1].start()

    def answer(dx):
        for k, at in enumerate(AROUND):
            if at[0] == dx:
                pair = AROUND.index((-at[0], -at[1]))
                copies[k].wait_recv()
                begin(pair, jnp.logical_not(ahead[pair]))

    answer(-1)
    answer(0)

    for level in range(GLEV):
        tall[pl.ds(level * 24, 8), :] = zero
        tall[pl.ds(level * 24 + 8, CX), :] = field[pl.ds(level * CX, CX), :]
    for r in range(HALO):
        tall[pl.ds(16 + r, GLEV, stride=24), :] = recv_rows[1, r]
    low_lanes = lane8 % 8 < 4
    for g in range(PACKS):
        edge[g, 0:8, :] = zero
        for at in range(2):
            edge[g, 8 * at + 8 : 8 * at + 16, :] = jnp.where(low_lanes, recv_cols[at, 1, g], recv_cols[at, 0, g])

    def spread(c, e):
        lane = lax.broadcasted_iota(jnp.int32, c.shape, 1)
        first_lane, last_lane = lane == 0, lane == CY - 1
        cr, cl = pltpu.roll(c, 1, 1), pltpu.roll(c, CY - 1, 1)
        er, el = pltpu.roll(e, 1, 1), pltpu.roll(e, CY - 1, 1)
        c_new = c + (jnp.where(first_lane, er, cr) + jnp.where(last_lane, el, cl))
        e_new = e + (jnp.where(first_lane, cr, er) + jnp.where(last_lane, cl, el))
        return c_new, e_new

    def sums(rows):
        at = [rows(k) for k in range(-HALO, HALO + 1)]
        return at[3], at[2] + at[4], at[1] + at[5], at[0] + at[6]

    for first in range(0, GLEV, BATCH):
        g, slots = first // PACK, [i % PACK for i in range(first, first + BATCH)]
        packed = sums(lambda k: edge[g, pl.ds(8 + k, 8), :])
        e = [jnp.concatenate([pltpu.roll(x, 128 - 8 * i, 1) if i else x for i in slots]) for x in packed]
        c = sums(
            lambda k: jnp.concatenate([tall[pl.ds((first + i) * 24 + 8 + k, 8), :] for i in range(BATCH)])
        )
        x, y = spread(c[0], e[0])
        x, y = spread(x + 3.0 * c[1], y + 3.0 * e[1])
        x, y = spread(x + (6.0 * c[0] + 3.0 * c[2]), y + (6.0 * e[0] + 3.0 * e[2]))
        result[pl.ds(first * CX, BATCH * CX), :] = 0.008 * (x + (3.0 * c[1] + c[3]))
    for a, b in zip(CUTS[:-1], CUTS[1:]):
        here, padded = pl.ds(a * CX, (b - a) * CX), pl.ds(PAD + a * CX, (b - a) * CX)
        change = [part for j in range(SETS) for part in split(temp[1, j, padded, :])]
        result[here, :] += dot(change, mean[...])

    answer(1)
    far = [jnp.where(low_lanes, recv_far[1, r], recv_far[0, r]) for r in range(2)]
    e1, e2 = (jnp.concatenate([pltpu.roll(x, 128 - 8 * g, 1) if g else x for g in range(GROUPS)]) for x in far)
    h1, h2, h3 = (recv_rows[0, r] for r in range(HALO))
    u, v = spread(h1, e1)
    w, _ = spread(u + h2, v + e2)
    for r, add in enumerate((3.0 * (w + h1) + h3, 3.0 * u + h2, h1)):
        result[pl.ds(r, GLEV, stride=CX), :] += 0.008 * add
    outs.append(pltpu.make_async_copy(result, dyn_hbm_out, out_sem.at[CHUNKS]))
    outs[-1].start()
    for copy in copies:
        copy.wait_send()
    for out in outs:
        out.wait()


def write(result, crm_new, dyn_out, crm_out, result_held, crm_held, sems):
    ins, outs = [], []
    for src, held, dst, n in ((result, result_held, dyn_out, 1), (crm_new, crm_held, crm_out, 4)):
        rows = src.shape[0] // n
        for c in range(n):
            part = pl.ds(c * rows, rows)
            ins.append(pltpu.make_async_copy(src.at[part], held.at[part], sems.at[0, len(ins)]))
            outs.append(pltpu.make_async_copy(held.at[part], dst.at[part], sems.at[1, len(outs)]))
    for load in ins:
        load.start()
    for load, store in zip(ins, outs):
        load.wait()
        store.start()
    for store in outs:
        store.wait()


def shards(sizes, dyn_field, crm_state, subcycles, dest_slot):
    hbm = pl.BlockSpec(memory_space=pltpu.HBM)
    state = (2, SETS, ROWS + 2 * PAD, 128)
    dyn_shape = jax.ShapeDtypeStruct((GROWS, CY), F32)
    crm_shape = jax.ShapeDtypeStruct((LEV * B_DEV, 128), F32)
    result, crm_new = pl.pallas_call(
        functools.partial(kernel, sizes),
        out_shape=(dyn_shape, crm_shape),
        in_specs=[hbm] * 4,
        out_specs=(hbm, hbm),
        scratch_shapes=[
            pltpu.VMEM((GROWS, CY), F32),
            pltpu.VMEM((LEV * B_DEV, 128), F32),
            pltpu.VMEM((GROWS, CY), F32),
            pltpu.VMEM((LEV * B_DEV, 128), F32),
            pltpu.VMEM((1, B_DEV), jnp.int32),
            pltpu.VMEM((1, B_DEV), jnp.int32),
            pltpu.VMEM((512, 256), BF16),
            pltpu.VMEM((256, 256), BF16),
            pltpu.VMEM((512, 128), BF16),
            pltpu.VMEM(state, F32),
            pltpu.VMEM(state, F32),
            pltpu.VMEM((SETS, ROWS, 128), F32),
            pltpu.VMEM((GLEV * 24, CY), F32),
            pltpu.VMEM((2, HALO, GLEV, CY), F32),
            pltpu.VMEM((2, HALO, GLEV, CY), F32),
            pltpu.VMEM((2, PACKS, 8, 128), F32),
            pltpu.VMEM((2, 2, PACKS, 8, 128), F32),
            pltpu.VMEM((2, 2, 8, 128), F32),
            pltpu.VMEM((2, 2, 8, 128), F32),
            pltpu.VMEM((PACKS, 24, 128), F32),
            pltpu.SemaphoreType.DMA((3,)),
            pltpu.SemaphoreType.DMA((CHUNKS,)),
            pltpu.SemaphoreType.DMA((CHUNKS + 1,)),
            pltpu.SemaphoreType.DMA((8,)),
            pltpu.SemaphoreType.DMA((8,)),
        ],
        compiler_params=pltpu.CompilerParams(
            collective_id=0, has_side_effects=True, vmem_limit_bytes=VMEM_BYTES
        ),
    )(
        subcycles.reshape(1, B_DEV),
        dest_slot.reshape(1, B_DEV),
        dyn_field.reshape(GROWS, CY),
        jnp.transpose(crm_state, (1, 0, 2)).reshape(LEV * B_DEV, 128),
    )
    dyn_out, crm_out = pl.pallas_call(
        write,
        out_shape=(dyn_shape, crm_shape),
        in_specs=[hbm] * 2,
        out_specs=(hbm, hbm),
        scratch_shapes=[
            pltpu.VMEM((GROWS, CY), F32),
            pltpu.VMEM((LEV * B_DEV, 128), F32),
            pltpu.SemaphoreType.DMA((2, 5)),
        ],
        compiler_params=pltpu.CompilerParams(vmem_limit_bytes=VMEM_BYTES),
    )(result, crm_new)
    crm_out = jnp.transpose(crm_out.reshape(LEV, B_DEV, 128), (1, 0, 2))
    return dyn_out.reshape(dyn_field.shape), crm_out


def solution(mesh):
    placed = (P(None, "ex", "ey"), P(("ex", "ey"), None, None), P(("ex", "ey")), P(("ex", "ey")))
    return jax.shard_map(
        functools.partial(shards, (mesh.shape["ex"], mesh.shape["ey"])),
        mesh=mesh,
        in_specs=placed,
        out_specs=(P(None, "ex", "ey"), P(("ex", "ey"), None, None)),
        check_vma=False,
    )
```

```python
import functools

import jax
import jax.numpy as jnp
import numpy as np
from jax import lax
from jax.experimental import pallas as pl
from jax.experimental.pallas import tpu as pltpu
from jax.sharding import PartitionSpec as P

F32 = jnp.float32
BF16 = jnp.bfloat16
MESH = pl.DeviceIdType.MESH

GLEV, LEV, COLS, CX, CY, B_DEV, MAXSUB = 72, 58, 64, 8, 128, 32, 12
PER_ROW = B_DEV // CX
STRIDE = CY // PER_ROW
ROWS = LEV * CX
GROWS = GLEV * CX
PAD = 8
SETS = PER_ROW // 2
CUTS = (0, 16, 30, 44, 58)
HALO = 3
PACK = 16
BATCH = 8
PACKS = (GLEV + PACK - 1) // PACK
GROUPS = GLEV // 8
CHUNKS = 2
VMEM_BYTES = 60 * 1024 * 1024
RATE = 0.3 * float(np.log2(np.e))
SCALED_T = RATE
SCALED_Q = 2.0
AROUND = [(1, 0), (1, -1), (1, 1), (0, -1), (0, 1), (-1, 0), (-1, -1), (-1, 1)]


def tables(step, pick, mean):
    def iotas(shape):
        return (lax.broadcasted_iota(jnp.int32, shape, d) for d in range(2))

    def where(flag, value):
        return jnp.where(flag, value, 0.0)

    row, col = iotas((256, 256))
    gap = (row - col) & (COLS - 1)
    same = row // COLS == col // COLS
    near = same & ((gap == 0) | (gap == 1) | (gap == COLS - 1))
    block = where(near, 1.0) - where(same & (row < 128), 1.0 / 128.0)
    step[0:256, :] = block.astype(BF16)
    step[256:512, :] = block.astype(BF16)
    block = where((row & 127) == STRIDE * (col // COLS), 1.0)
    pick[...] = block.astype(BF16)
    row, col = iotas((256, 128))
    for j in range(SETS):
        block = where(col == STRIDE * (2 * j + (row & 127) // COLS), 1.0 / COLS)
        mean[256 * j : 256 * j + 256, :] = block.astype(BF16)


def split(x):
    high = x.astype(BF16)
    return high, (x - high.astype(F32)).astype(BF16)


def dot(terms, m):
    return jnp.dot(jnp.concatenate(terms, axis=1), m, preferred_element_type=F32)


def kernel(
    sizes, sub_hbm, slot_hbm, dyn_hbm, crm_hbm,
    dyn_hbm_out, crm_hbm_out,
    result, crm_new, field, crm, sub, slot, step, pick, mean, temp, moist, pull,
    tall, send_rows, recv_rows, send_cols, recv_cols, send_far, recv_far, edge,
    load_sem, in_sem, out_sem, send_sem, recv_sem,
):
    nex, ney = sizes
    ex, ey = lax.axis_index("ex"), lax.axis_index("ey")

    def device(dx, dy):
        return lax.rem(ex + dx + nex, nex), lax.rem(ey + dy + ney, ney)

    def answers(dx):
        return ex == 0 if dx == -1 else ex < 0

    def awaited(dx):
        return ex == nex - 1 if dx == 1 else ex < 0

    cloud_first = (ex < nex // 4) & (ex + ey > 0)

    barrier = pltpu.get_barrier_semaphore()
    for at in AROUND:
        @pl.when(jnp.logical_not(awaited(at[0])))
        def _():
            pl.semaphore_signal(barrier, inc=1, device_id=device(*at), device_id_type=MESH)

    small = [(dyn_hbm, field), (sub_hbm, sub), (slot_hbm, slot)]
    small = [pltpu.make_async_copy(src, dst, load_sem.at[i]) for i, (src, dst) in enumerate(small)]
    for copy in small:
        copy.start()
    loads = []
    per = LEV * B_DEV // CHUNKS
    for c in range(CHUNKS):
        part = pl.ds(c * per, per)
        loads.append(pltpu.make_async_copy(crm_hbm.at[part], crm.at[part], in_sem.at[c]))
        loads[-1].start()

    lane8 = lax.broadcasted_iota(jnp.int32, (8, 128), 1)
    row8 = lax.broadcasted_iota(jnp.int32, (8, 128), 0)
    left8 = lane8 < COLS
    zero = jnp.zeros((8, 128), F32)

    small[0].wait()
    for r in range(HALO):
        send_rows[1, r] = field[pl.ds(CX - 1 - r, GLEV, stride=CX), :]
    for r in range(HALO):
        send_rows[0, r] = field[pl.ds(r, GLEV, stride=CX), :]

    copies = []
    for k, (dx, dy) in enumerate(AROUND):
        side = (dy + 1) // 2
        if dy == 0:
            src, dst = send_rows.at[(dx + 1) // 2], recv_rows.at[(1 - dx) // 2]
        elif dx == 0:
            src, dst = send_cols.at[side], recv_cols.at[1 - side]
        else:
            src, dst = send_far.at[(dx + 1) // 2, side], recv_far.at[(1 - dx) // 2, 1 - side]
        copies.append(
            pltpu.make_async_remote_copy(
                src_ref=src,
                dst_ref=dst,
                send_sem=send_sem.at[k],
                recv_sem=recv_sem.at[k],
                device_id=device(dx, dy),
                device_id_type=MESH,
            )
        )

    for end in range(2):
        for r in range(2):
            head, tail = zero, zero
            for g in range(GROUPS):
                tile = send_rows[end, r, 8 * g : 8 * g + 8, :]
                tile = pltpu.roll(tile, 8 * g, 1) if g else tile
                head = jnp.where(lane8 // 8 == g, tile, head)
                tail = jnp.where(lane8 // 8 == (g - 1) % 16, tile, tail)
            send_far[end, 0, r] = head
            send_far[end, 1, r] = tail
    for g in range(PACKS):
        head, tail = zero, zero
        for i in range(min(PACK, GLEV - g * PACK)):
            tile = field[pl.ds((g * PACK + i) * CX, CX), :]
            tile = pltpu.roll(tile, 8 * i, 1) if i else tile
            head = jnp.where(lane8 // 8 == i, tile, head)
            tail = jnp.where(lane8 // 8 == (i - 1) % PACK, tile, tail)
        send_cols[0, g] = head
        send_cols[1, g] = tail

    def exchange():
        n = len(AROUND) - jnp.where(ex == 0, 3, 0)
        pl.semaphore_wait(barrier, n)
        for (dx, dy), copy in zip(AROUND, copies):
            pl.when(jnp.logical_not(answers(dx)))(copy.start)

    pl.when(jnp.logical_not(cloud_first))(exchange)

    small[1].wait()
    small[2].wait()
    active = jnp.where(slot[...] >= 0, sub[...], 0).astype(F32)
    lane32 = lax.broadcasted_iota(jnp.int32, (CX, B_DEV), 1)
    row32 = lax.broadcasted_iota(jnp.int32, (CX, B_DEV), 0)
    spread_out = jnp.broadcast_to(active, (CX, B_DEV))
    counts = []
    for k in range(PER_ROW):
        own = jnp.where(lane32 == PER_ROW * row32 + k, spread_out, 0.0)
        counts.append(jnp.sum(own, axis=1, keepdims=True))
    counts = [jnp.where(left8, counts[2 * j], counts[2 * j + 1]) for j in range(SETS)]

    for side in range(2):
        for j in range(SETS):
            for buf in (temp, moist):
                buf[side, j, 0:PAD, :] = zero
                buf[side, j, PAD + ROWS : PAD + ROWS + PAD, :] = zero

    tables(step, pick, mean)
    for a, b in zip(CUTS[:-1], CUTS[1:]):
        here = pl.ds(a * CX, (b - a) * CX)
        wide = (0.1 * SCALED_T) * dot(split(field[here, :]), pick[...])
        for j in range(SETS):
            pull[j, here, :] = wide[:, 128 * j : 128 * j + 128]

    def warm_and_moist(j, level):
        one, two = (crm[pl.ds(level * B_DEV + 2 * j + i, CX, stride=PER_ROW), :] for i in range(2))
        t = jnp.where(left8, one, pltpu.roll(two, COLS, 1))
        q = jnp.where(left8, pltpu.roll(one, COLS, 1), two)
        return t, q

    for load in loads:
        load.wait()
    for level in range(LEV):
        for j in range(SETS):
            t, q = warm_and_moist(j, level)
            temp[0, j, pl.ds(PAD + level * CX, CX), :] = SCALED_T * t
            moist[0, j, pl.ds(PAD + level * CX, CX), :] = SCALED_Q * q

    def substep(n, old, new):
        for j in range(SETS):
            on = n < counts[j]
            for a, b in zip(CUTS[:-1], CUTS[1:]):
                base, rows = PAD + a * CX, (b - a) * CX
                here, up, down = (pl.ds(base + s, rows) for s in (0, CX, -CX))
                t, q = temp[old, j, here, :], moist[old, j, here, :]
                (t1, t2), (q1, q2) = split(t), split(q)
                across = dot([t1, q1, t2, q2], step[...])
                vt = temp[old, j, up, :] + temp[old, j, down, :]
                vq = moist[old, j, up, :] + moist[old, j, down, :]
                e = jnp.maximum(q - jnp.exp2(t), 0.0)
                t_new = 0.2 * (across[:, :128] + vt) + (pull[j, pl.ds(a * CX, rows), :] + (0.125 * SCALED_T) * e)
                q_new = 0.2 * (across[:, 128:] + vq) - 0.5 * e
                mask = jnp.concatenate([on] * (b - a), axis=0)
                temp[new, j, here, :] = jnp.where(mask, t_new, t)
                moist[new, j, here, :] = jnp.where(mask, q_new, q)

    @pl.loop(0, MAXSUB // 2)
    def _(n):
        now = (2 * n).astype(F32)
        substep(now, 0, 1)
        substep(now + 1.0, 1, 0)

    outs = []
    for c in range(CHUNKS):
        for level in range(c * LEV // CHUNKS, (c + 1) * LEV // CHUNKS):
            for j in range(SETS):
                own = pl.ds(PAD + level * CX, CX)
                t = (1.0 / SCALED_T) * temp[0, j, own, :]
                q = (1.0 / SCALED_Q) * moist[0, j, own, :]
                temp[1, j, own, :] = t - warm_and_moist(j, level)[0]
                at = [pl.ds(level * B_DEV + 2 * j + i, CX, stride=PER_ROW) for i in range(2)]
                crm_new[at[0], :] = jnp.where(left8, t, pltpu.roll(q, COLS, 1))
                crm_new[at[1], :] = jnp.where(left8, pltpu.roll(t, COLS, 1), q)
        part = pl.ds(c * per, per)
        outs.append(pltpu.make_async_copy(crm_new.at[part], crm_hbm_out.at[part], out_sem.at[c]))
        outs[-1].start()

    pl.when(cloud_first)(exchange)

    def spread(c, e):
        lane = lax.broadcasted_iota(jnp.int32, c.shape, 1)
        first_lane, last_lane = lane == 0, lane == CY - 1
        cr, cl = pltpu.roll(c, 1, 1), pltpu.roll(c, CY - 1, 1)
        er, el = pltpu.roll(e, 1, 1), pltpu.roll(e, CY - 1, 1)
        c_new = c + (jnp.where(first_lane, er, cr) + jnp.where(last_lane, el, cl))
        e_new = e + (jnp.where(first_lane, cr, er) + jnp.where(last_lane, cl, el))
        return c_new, e_new

    for level in range(GLEV):
        tall[pl.ds(level * 24, 8), :] = zero
        tall[pl.ds(level * 24 + 8, CX), :] = field[pl.ds(level * CX, CX), :]
        tall[pl.ds(level * 24 + 16, 8), :] = zero
    for start in range(0, GLEV, BATCH):
        at = [
            jnp.concatenate([tall[pl.ds((start + i) * 24 + 8 + k, 8), :] for i in range(BATCH)])
            for k in range(-HALO, HALO + 1)
        ]
        c0, c1, c2, c3 = at[3], at[2] + at[4], at[1] + at[5], at[0] + at[6]
        x, y = spread(c0, jnp.zeros_like(c0))
        x, y = spread(x + 3.0 * c1, y)
        x, y = spread(x + (6.0 * c0 + 3.0 * c2), y)
        result[pl.ds(start * CX, BATCH * CX), :] = 0.008 * (x + (3.0 * c1 + c3))
    for a, b in zip(CUTS[:-1], CUTS[1:]):
        here, padded = pl.ds(a * CX, (b - a) * CX), pl.ds(PAD + a * CX, (b - a) * CX)
        change = [part for j in range(SETS) for part in split(temp[1, j, padded, :])]
        result[here, :] += dot(change, mean[...])

    def take(dx):
        for k, at in enumerate(AROUND):
            if at[0] == dx:
                copies[k].wait_recv()

    low_lanes = lane8 % 8 < 4
    for side in range(2):
        edge[side, 0:8, :] = zero
        edge[side, 16:24, :] = zero

    take(0)
    for g in range(PACKS):
        sides = []
        for side in range(2):
            halo = recv_cols[side, g]
            beyond = (lane8 % 8 >= 5) if side == 0 else (lane8 % 8 < 3)
            valid = (lane8 % 8 >= 5) | (lane8 % 8 < 3)
            halo = jnp.where(beyond, halo, 0.0)
            edge[side, 8:16, :] = halo
            at = [edge[side, 8 + k : 16 + k, :] for k in range(-HALO, HALO + 1)]
            c0, c1, c2, c3 = halo, at[2] + at[4], at[1] + at[5], at[0] + at[6]

            def near(x):
                return x + jnp.where(valid, pltpu.roll(x, 1, 1) + pltpu.roll(x, CY - 1, 1), 0.0)

            x = near(c0)
            x = near(x + 3.0 * c1)
            x = near(x + (6.0 * c0 + 3.0 * c2))
            sides.append(0.008 * x)
        both = jnp.where(low_lanes, sides[0], sides[1])
        levels = range(g * PACK, min(GLEV, g * PACK + PACK))
        add = jnp.concatenate([pltpu.roll(both, (128 - 8 * (i % PACK)) % 128, 1) if i % PACK else both for i in levels])
        lane = lax.broadcasted_iota(jnp.int32, add.shape, 1)
        own = pl.ds(levels[0] * CX, len(levels) * CX)
        result[own, :] += jnp.where((lane < 3) | (lane >= CY - 3), add, 0.0)

    for dx in (-1, 1):
        take(dx)
        end = (1 - dx) // 2
        far = [jnp.where(low_lanes, recv_far[end, 1, r], recv_far[end, 0, r]) for r in range(2)]
        e1, e2 = (
            jnp.concatenate([pltpu.roll(x, 128 - 8 * g, 1) if g else x for g in range(GROUPS)]) for x in far
        )
        h1, h2, h3 = (recv_rows[end, r] for r in range(HALO))
        u, v = spread(h1, e1)
        w, _ = spread(u + h2, v + e2)
        for r, add in enumerate((3.0 * (w + h1) + h3, 3.0 * u + h2, h1)):
            result[pl.ds(CX - 1 - r if end else r, GLEV, stride=CX), :] += 0.008 * add
        for (ax, _), copy in zip(AROUND, copies):
            if ax == -dx:
                pl.when(answers(ax))(copy.start)
    outs.append(pltpu.make_async_copy(result, dyn_hbm_out, out_sem.at[CHUNKS]))
    outs[-1].start()
    for copy in copies:
        copy.wait_send()
    for out in outs:
        out.wait()


def write(result, crm_new, dyn_out, crm_out, result_held, crm_held, sems):
    ins, outs = [], []
    for src, held, dst, n in ((result, result_held, dyn_out, 1), (crm_new, crm_held, crm_out, 4)):
        rows = src.shape[0] // n
        for c in range(n):
            part = pl.ds(c * rows, rows)
            ins.append(pltpu.make_async_copy(src.at[part], held.at[part], sems.at[0, len(ins)]))
            outs.append(pltpu.make_async_copy(held.at[part], dst.at[part], sems.at[1, len(outs)]))
    for load in ins:
        load.start()
    for load, store in zip(ins, outs):
        load.wait()
        store.start()
    for store in outs:
        store.wait()


def shards(sizes, dyn_field, crm_state, subcycles, dest_slot):
    hbm = pl.BlockSpec(memory_space=pltpu.HBM)
    state = (2, SETS, ROWS + 2 * PAD, 128)
    dyn_shape = jax.ShapeDtypeStruct((GROWS, CY), F32)
    crm_shape = jax.ShapeDtypeStruct((LEV * B_DEV, 128), F32)
    result, crm_new = pl.pallas_call(
        functools.partial(kernel, sizes),
        out_shape=(dyn_shape, crm_shape),
        in_specs=[hbm] * 4,
        out_specs=(hbm, hbm),
        scratch_shapes=[
            pltpu.VMEM((GROWS, CY), F32),
            pltpu.VMEM((LEV * B_DEV, 128), F32),
            pltpu.VMEM((GROWS, CY), F32),
            pltpu.VMEM((LEV * B_DEV, 128), F32),
            pltpu.VMEM((1, B_DEV), jnp.int32),
            pltpu.VMEM((1, B_DEV), jnp.int32),
            pltpu.VMEM((512, 256), BF16),
            pltpu.VMEM((256, 256), BF16),
            pltpu.VMEM((512, 128), BF16),
            pltpu.VMEM(state, F32),
            pltpu.VMEM(state, F32),
            pltpu.VMEM((SETS, ROWS, 128), F32),
            pltpu.VMEM((GLEV * 24, CY), F32),
            pltpu.VMEM((2, HALO, GLEV, CY), F32),
            pltpu.VMEM((2, HALO, GLEV, CY), F32),
            pltpu.VMEM((2, PACKS, 8, 128), F32),
            pltpu.VMEM((2, PACKS, 8, 128), F32),
            pltpu.VMEM((2, 2, 2, 8, 128), F32),
            pltpu.VMEM((2, 2, 2, 8, 128), F32),
            pltpu.VMEM((2, 24, 128), F32),
            pltpu.SemaphoreType.DMA((3,)),
            pltpu.SemaphoreType.DMA((CHUNKS,)),
            pltpu.SemaphoreType.DMA((CHUNKS + 1,)),
            pltpu.SemaphoreType.DMA((8,)),
            pltpu.SemaphoreType.DMA((8,)),
        ],
        compiler_params=pltpu.CompilerParams(
            collective_id=0, has_side_effects=True, vmem_limit_bytes=VMEM_BYTES
        ),
    )(
        subcycles.reshape(1, B_DEV),
        dest_slot.reshape(1, B_DEV),
        dyn_field.reshape(GROWS, CY),
        jnp.transpose(crm_state, (1, 0, 2)).reshape(LEV * B_DEV, 128),
    )
    dyn_out, crm_out = pl.pallas_call(
        write,
        out_shape=(dyn_shape, crm_shape),
        in_specs=[hbm] * 2,
        out_specs=(hbm, hbm),
        scratch_shapes=[
            pltpu.VMEM((GROWS, CY), F32),
            pltpu.VMEM((LEV * B_DEV, 128), F32),
            pltpu.SemaphoreType.DMA((2, 5)),
        ],
        compiler_params=pltpu.CompilerParams(vmem_limit_bytes=VMEM_BYTES),
    )(result, crm_new)
    crm_out = jnp.transpose(crm_out.reshape(LEV, B_DEV, 128), (1, 0, 2))
    return dyn_out.reshape(dyn_field.shape), crm_out


def solution(mesh):
    placed = (P(None, "ex", "ey"), P(("ex", "ey"), None, None), P(("ex", "ey")), P(("ex", "ey")))
    return jax.shard_map(
        functools.partial(shards, (mesh.shape["ex"], mesh.shape["ey"])),
        mesh=mesh,
        in_specs=placed,
        out_specs=(P(None, "ex", "ey"), P(("ex", "ey"), None, None)),
        check_vma=False,
    )
```

```python
import functools

import jax
import jax.numpy as jnp
import numpy as np
from jax import lax
from jax.experimental import pallas as pl
from jax.experimental.pallas import tpu as pltpu
from jax.sharding import PartitionSpec as P

F32 = jnp.float32
BF16 = jnp.bfloat16
MESH = pl.DeviceIdType.MESH

GLEV, LEV, COLS, CX, CY, B_DEV, MAXSUB = 72, 58, 64, 8, 128, 32, 12
PER_ROW = B_DEV // CX
STRIDE = CY // PER_ROW
ROWS = LEV * CX
GROWS = GLEV * CX
PAD = 8
SETS = PER_ROW // 2
CUTS = (0, 16, 30, 44, 58)
HALO = 3
PACK = 16
BATCH = 8
PACKS = (GLEV + PACK - 1) // PACK
GROUPS = GLEV // 8
CHUNKS = 2
VMEM_BYTES = 60 * 1024 * 1024
RATE = 0.3 * float(np.log2(np.e))
SCALED_T = RATE
SCALED_Q = 2.0
AROUND = [(0, 1), (1, 1), (-1, 1), (0, -1), (1, -1), (-1, -1), (1, 0), (-1, 0)]


def tables(step, pick, mean):
    def iotas(shape):
        return (lax.broadcasted_iota(jnp.int32, shape, d) for d in range(2))

    def where(flag, value):
        return jnp.where(flag, value, 0.0)

    row, col = iotas((256, 256))
    gap = (row - col) & (COLS - 1)
    same = row // COLS == col // COLS
    near = same & ((gap == 0) | (gap == 1) | (gap == COLS - 1))
    block = where(near, 1.0) - where(same & (row < 128), 1.0 / 128.0)
    step[0:256, :] = block.astype(BF16)
    step[256:512, :] = block.astype(BF16)
    block = where((row & 127) == STRIDE * (col // COLS), 1.0)
    pick[...] = block.astype(BF16)
    row, col = iotas((256, 128))
    for j in range(SETS):
        block = where(col == STRIDE * (2 * j + (row & 127) // COLS), 1.0 / COLS)
        mean[256 * j : 256 * j + 256, :] = block.astype(BF16)


def split(x):
    high = x.astype(BF16)
    return high, (x - high.astype(F32)).astype(BF16)


def dot(terms, m):
    return jnp.dot(jnp.concatenate(terms, axis=1), m, preferred_element_type=F32)


def kernel(
    sizes, sub_hbm, slot_hbm, dyn_hbm, crm_hbm,
    dyn_hbm_out, crm_hbm_out,
    result, crm_new, field, crm, sub, slot, step, pick, mean, temp, moist, pull,
    tall, send_rows, recv_rows, send_cols, recv_cols, send_far, recv_far, edge,
    load_sem, in_sem, out_sem, send_sem, recv_sem,
):
    nex, ney = sizes
    ex, ey = lax.axis_index("ex"), lax.axis_index("ey")

    def device(dx, dy):
        return lax.rem(ex + dx + nex, nex), lax.rem(ey + dy + ney, ney)

    first = (ex == 0) & (ey == 0)
    last_ey = ey == ney - 1

    def answers(dx, dy):
        x, y = device(dx, dy)
        to_first = (x == 0) & (y == 0) & jnp.logical_not(last_ey)
        return to_first | (ey == 0) if dy == -1 else to_first

    def awaited(dx, dy):
        return last_ey | first if dy == 1 else first if dy == 0 else first & (ey > 0)

    barrier = pltpu.get_barrier_semaphore()
    for at in AROUND:
        @pl.when(jnp.logical_not(awaited(*at)))
        def _():
            pl.semaphore_signal(barrier, inc=1, device_id=device(*at), device_id_type=MESH)

    small = [(dyn_hbm, field), (sub_hbm, sub), (slot_hbm, slot)]
    small = [pltpu.make_async_copy(src, dst, load_sem.at[i]) for i, (src, dst) in enumerate(small)]
    for copy in small:
        copy.start()
    loads = []
    per = LEV * B_DEV // CHUNKS
    for c in range(CHUNKS):
        part = pl.ds(c * per, per)
        loads.append(pltpu.make_async_copy(crm_hbm.at[part], crm.at[part], in_sem.at[c]))
        loads[-1].start()

    lane8 = lax.broadcasted_iota(jnp.int32, (8, 128), 1)
    row8 = lax.broadcasted_iota(jnp.int32, (8, 128), 0)
    left8 = lane8 < COLS
    zero = jnp.zeros((8, 128), F32)

    small[0].wait()
    for r in range(HALO):
        send_rows[1, r] = field[pl.ds(CX - 1 - r, GLEV, stride=CX), :]
    for r in range(HALO):
        send_rows[0, r] = field[pl.ds(r, GLEV, stride=CX), :]

    copies = []
    for k, (dx, dy) in enumerate(AROUND):
        side = (dy + 1) // 2
        if dy == 0:
            src, dst = send_rows.at[(dx + 1) // 2], recv_rows.at[(1 - dx) // 2]
        elif dx == 0:
            src, dst = send_cols.at[side], recv_cols.at[1 - side]
        else:
            src, dst = send_far.at[(dx + 1) // 2, side], recv_far.at[(1 - dx) // 2, 1 - side]
        copies.append(
            pltpu.make_async_remote_copy(
                src_ref=src,
                dst_ref=dst,
                send_sem=send_sem.at[k],
                recv_sem=recv_sem.at[k],
                device_id=device(dx, dy),
                device_id_type=MESH,
            )
        )

    for end in range(2):
        for r in range(2):
            head, tail = zero, zero
            for g in range(GROUPS):
                tile = send_rows[end, r, 8 * g : 8 * g + 8, :]
                tile = pltpu.roll(tile, 8 * g, 1) if g else tile
                head = jnp.where(lane8 // 8 == g, tile, head)
                tail = jnp.where(lane8 // 8 == (g - 1) % 16, tile, tail)
            send_far[end, 0, r] = head
            send_far[end, 1, r] = tail
    for g in range(PACKS):
        head, tail = zero, zero
        for i in range(min(PACK, GLEV - g * PACK)):
            tile = field[pl.ds((g * PACK + i) * CX, CX), :]
            tile = pltpu.roll(tile, 8 * i, 1) if i else tile
            head = jnp.where(lane8 // 8 == i, tile, head)
            tail = jnp.where(lane8 // 8 == (i - 1) % PACK, tile, tail)
        send_cols[0, g] = head
        send_cols[1, g] = tail

    n_mutual = sum(jnp.where(answers(*at), 0, 1) for at in AROUND)
    pl.semaphore_wait(barrier, n_mutual)
    for at, copy in zip(AROUND, copies):
        pl.when(jnp.logical_not(answers(*at)))(copy.start)

    small[1].wait()
    small[2].wait()
    active = jnp.where(slot[...] >= 0, sub[...], 0).astype(F32)
    lane32 = lax.broadcasted_iota(jnp.int32, (CX, B_DEV), 1)
    row32 = lax.broadcasted_iota(jnp.int32, (CX, B_DEV), 0)
    spread_out = jnp.broadcast_to(active, (CX, B_DEV))
    counts = []
    for k in range(PER_ROW):
        own = jnp.where(lane32 == PER_ROW * row32 + k, spread_out, 0.0)
        counts.append(jnp.sum(own, axis=1, keepdims=True))
    counts = [jnp.where(left8, counts[2 * j], counts[2 * j + 1]) for j in range(SETS)]

    for side in range(2):
        for j in range(SETS):
            for buf in (temp, moist):
                buf[side, j, 0:PAD, :] = zero
                buf[side, j, PAD + ROWS : PAD + ROWS + PAD, :] = zero

    tables(step, pick, mean)
    for a, b in zip(CUTS[:-1], CUTS[1:]):
        here = pl.ds(a * CX, (b - a) * CX)
        wide = (0.1 * SCALED_T) * dot(split(field[here, :]), pick[...])
        for j in range(SETS):
            pull[j, here, :] = wide[:, 128 * j : 128 * j + 128]

    def warm_and_moist(j, level):
        one, two = (crm[pl.ds(level * B_DEV + 2 * j + i, CX, stride=PER_ROW), :] for i in range(2))
        t = jnp.where(left8, one, pltpu.roll(two, COLS, 1))
        q = jnp.where(left8, pltpu.roll(one, COLS, 1), two)
        return t, q

    for load in loads:
        load.wait()
    for level in range(LEV):
        for j in range(SETS):
            t, q = warm_and_moist(j, level)
            temp[0, j, pl.ds(PAD + level * CX, CX), :] = SCALED_T * t
            moist[0, j, pl.ds(PAD + level * CX, CX), :] = SCALED_Q * q

    def substep(n, old, new):
        for j in range(SETS):
            on = n < counts[j]
            for a, b in zip(CUTS[:-1], CUTS[1:]):
                base, rows = PAD + a * CX, (b - a) * CX
                here, up, down = (pl.ds(base + s, rows) for s in (0, CX, -CX))
                t, q = temp[old, j, here, :], moist[old, j, here, :]
                (t1, t2), (q1, q2) = split(t), split(q)
                across = dot([t1, q1, t2, q2], step[...])
                vt = temp[old, j, up, :] + temp[old, j, down, :]
                vq = moist[old, j, up, :] + moist[old, j, down, :]
                e = jnp.maximum(q - jnp.exp2(t), 0.0)
                t_new = 0.2 * (across[:, :128] + vt) + (pull[j, pl.ds(a * CX, rows), :] + (0.125 * SCALED_T) * e)
                q_new = 0.2 * (across[:, 128:] + vq) - 0.5 * e
                mask = jnp.concatenate([on] * (b - a), axis=0)
                temp[new, j, here, :] = jnp.where(mask, t_new, t)
                moist[new, j, here, :] = jnp.where(mask, q_new, q)

    @pl.loop(0, MAXSUB // 2)
    def _(n):
        now = (2 * n).astype(F32)
        substep(now, 0, 1)
        substep(now + 1.0, 1, 0)

    outs = []
    for c in range(CHUNKS):
        for level in range(c * LEV // CHUNKS, (c + 1) * LEV // CHUNKS):
            for j in range(SETS):
                own = pl.ds(PAD + level * CX, CX)
                t = (1.0 / SCALED_T) * temp[0, j, own, :]
                q = (1.0 / SCALED_Q) * moist[0, j, own, :]
                temp[1, j, own, :] = t - warm_and_moist(j, level)[0]
                at = [pl.ds(level * B_DEV + 2 * j + i, CX, stride=PER_ROW) for i in range(2)]
                crm_new[at[0], :] = jnp.where(left8, t, pltpu.roll(q, COLS, 1))
                crm_new[at[1], :] = jnp.where(left8, pltpu.roll(t, COLS, 1), q)
        part = pl.ds(c * per, per)
        outs.append(pltpu.make_async_copy(crm_new.at[part], crm_hbm_out.at[part], out_sem.at[c]))
        outs[-1].start()

    def spread(c, e):
        lane = lax.broadcasted_iota(jnp.int32, c.shape, 1)
        first_lane, last_lane = lane == 0, lane == CY - 1
        cr, cl = pltpu.roll(c, 1, 1), pltpu.roll(c, CY - 1, 1)
        er, el = pltpu.roll(e, 1, 1), pltpu.roll(e, CY - 1, 1)
        c_new = c + (jnp.where(first_lane, er, cr) + jnp.where(last_lane, el, cl))
        e_new = e + (jnp.where(first_lane, cr, er) + jnp.where(last_lane, cl, el))
        return c_new, e_new

    for level in range(GLEV):
        tall[pl.ds(level * 24, 8), :] = zero
        tall[pl.ds(level * 24 + 8, CX), :] = field[pl.ds(level * CX, CX), :]
        tall[pl.ds(level * 24 + 16, 8), :] = zero
    for start in range(0, GLEV, BATCH):
        at = [
            jnp.concatenate([tall[pl.ds((start + i) * 24 + 8 + k, 8), :] for i in range(BATCH)])
            for k in range(-HALO, HALO + 1)
        ]
        c0, c1, c2, c3 = at[3], at[2] + at[4], at[1] + at[5], at[0] + at[6]
        x, y = spread(c0, jnp.zeros_like(c0))
        x, y = spread(x + 3.0 * c1, y)
        x, y = spread(x + (6.0 * c0 + 3.0 * c2), y)
        result[pl.ds(start * CX, BATCH * CX), :] = 0.008 * (x + (3.0 * c1 + c3))
    for a, b in zip(CUTS[:-1], CUTS[1:]):
        here, padded = pl.ds(a * CX, (b - a) * CX), pl.ds(PAD + a * CX, (b - a) * CX)
        change = [part for j in range(SETS) for part in split(temp[1, j, padded, :])]
        result[here, :] += dot(change, mean[...])

    def take(k):
        copies[k].wait_recv()
        back = AROUND.index((-AROUND[k][0], -AROUND[k][1]))
        pl.when(answers(*AROUND[back]))(copies[back].start)

    def add_rows(end, h1, h2, h3, e1, e2):
        u, v = spread(h1, e1)
        w, _ = spread(u + h2, v + e2)
        for r, add in enumerate((3.0 * (w + h1) + h3, 3.0 * u + h2, h1)):
            result[pl.ds(CX - 1 - r if end else r, GLEV, stride=CX), :] += 0.008 * add

    nothing = jnp.zeros((GLEV, CY), F32)
    for dx in (-1, 1):
        take(AROUND.index((dx, 0)))
        end = (1 - dx) // 2
        add_rows(end, *(recv_rows[end, r] for r in range(HALO)), nothing, nothing)

    low_lanes = lane8 % 8 < 4
    for side in range(2):
        edge[side, 0:8, :] = zero
        edge[side, 16:24, :] = zero

    for dy in (-1, 1):
        for k, at in enumerate(AROUND):
            if at[1] == dy:
                take(k)
    for g in range(PACKS):
        sides = []
        for side in range(2):
            halo = recv_cols[side, g]
            beyond = (lane8 % 8 >= 5) if side == 0 else (lane8 % 8 < 3)
            valid = (lane8 % 8 >= 5) | (lane8 % 8 < 3)
            halo = jnp.where(beyond, halo, 0.0)
            edge[side, 8:16, :] = halo
            at = [edge[side, 8 + k : 16 + k, :] for k in range(-HALO, HALO + 1)]
            c0, c1, c2, c3 = halo, at[2] + at[4], at[1] + at[5], at[0] + at[6]

            def near(x):
                return x + jnp.where(valid, pltpu.roll(x, 1, 1) + pltpu.roll(x, CY - 1, 1), 0.0)

            x = near(c0)
            x = near(x + 3.0 * c1)
            x = near(x + (6.0 * c0 + 3.0 * c2))
            sides.append(0.008 * x)
        both = jnp.where(low_lanes, sides[0], sides[1])
        levels = range(g * PACK, min(GLEV, g * PACK + PACK))
        add = jnp.concatenate([pltpu.roll(both, (128 - 8 * (i % PACK)) % 128, 1) if i % PACK else both for i in levels])
        lane = lax.broadcasted_iota(jnp.int32, add.shape, 1)
        own = pl.ds(levels[0] * CX, len(levels) * CX)
        result[own, :] += jnp.where((lane < 3) | (lane >= CY - 3), add, 0.0)

    for end in range(2):
        far = [jnp.where(low_lanes, recv_far[end, 1, r], recv_far[end, 0, r]) for r in range(2)]
        e1, e2 = (
            jnp.concatenate([pltpu.roll(x, 128 - 8 * g, 1) if g else x for g in range(GROUPS)]) for x in far
        )
        add_rows(end, nothing, nothing, nothing, e1, e2)
    outs.append(pltpu.make_async_copy(result, dyn_hbm_out, out_sem.at[CHUNKS]))
    outs[-1].start()
    for copy in copies:
        copy.wait_send()
    for out in outs:
        out.wait()


def write(result, crm_new, dyn_out, crm_out, result_held, crm_held, sems):
    ins, outs = [], []
    for src, held, dst, n in ((result, result_held, dyn_out, 1), (crm_new, crm_held, crm_out, 4)):
        rows = src.shape[0] // n
        for c in range(n):
            part = pl.ds(c * rows, rows)
            ins.append(pltpu.make_async_copy(src.at[part], held.at[part], sems.at[0, len(ins)]))
            outs.append(pltpu.make_async_copy(held.at[part], dst.at[part], sems.at[1, len(outs)]))
    for load in ins:
        load.start()
    for load, store in zip(ins, outs):
        load.wait()
        store.start()
    for store in outs:
        store.wait()


def shards(sizes, dyn_field, crm_state, subcycles, dest_slot):
    hbm = pl.BlockSpec(memory_space=pltpu.HBM)
    state = (2, SETS, ROWS + 2 * PAD, 128)
    dyn_shape = jax.ShapeDtypeStruct((GROWS, CY), F32)
    crm_shape = jax.ShapeDtypeStruct((LEV * B_DEV, 128), F32)
    result, crm_new = pl.pallas_call(
        functools.partial(kernel, sizes),
        out_shape=(dyn_shape, crm_shape),
        in_specs=[hbm] * 4,
        out_specs=(hbm, hbm),
        scratch_shapes=[
            pltpu.VMEM((GROWS, CY), F32),
            pltpu.VMEM((LEV * B_DEV, 128), F32),
            pltpu.VMEM((GROWS, CY), F32),
            pltpu.VMEM((LEV * B_DEV, 128), F32),
            pltpu.VMEM((1, B_DEV), jnp.int32),
            pltpu.VMEM((1, B_DEV), jnp.int32),
            pltpu.VMEM((512, 256), BF16),
            pltpu.VMEM((256, 256), BF16),
            pltpu.VMEM((512, 128), BF16),
            pltpu.VMEM(state, F32),
            pltpu.VMEM(state, F32),
            pltpu.VMEM((SETS, ROWS, 128), F32),
            pltpu.VMEM((GLEV * 24, CY), F32),
            pltpu.VMEM((2, HALO, GLEV, CY), F32),
            pltpu.VMEM((2, HALO, GLEV, CY), F32),
            pltpu.VMEM((2, PACKS, 8, 128), F32),
            pltpu.VMEM((2, PACKS, 8, 128), F32),
            pltpu.VMEM((2, 2, 2, 8, 128), F32),
            pltpu.VMEM((2, 2, 2, 8, 128), F32),
            pltpu.VMEM((2, 24, 128), F32),
            pltpu.SemaphoreType.DMA((3,)),
            pltpu.SemaphoreType.DMA((CHUNKS,)),
            pltpu.SemaphoreType.DMA((CHUNKS + 1,)),
            pltpu.SemaphoreType.DMA((8,)),
            pltpu.SemaphoreType.DMA((8,)),
        ],
        compiler_params=pltpu.CompilerParams(
            collective_id=0, has_side_effects=True, vmem_limit_bytes=VMEM_BYTES
        ),
    )(
        subcycles.reshape(1, B_DEV),
        dest_slot.reshape(1, B_DEV),
        dyn_field.reshape(GROWS, CY),
        jnp.transpose(crm_state, (1, 0, 2)).reshape(LEV * B_DEV, 128),
    )
    dyn_out, crm_out = pl.pallas_call(
        write,
        out_shape=(dyn_shape, crm_shape),
        in_specs=[hbm] * 2,
        out_specs=(hbm, hbm),
        scratch_shapes=[
            pltpu.VMEM((GROWS, CY), F32),
            pltpu.VMEM((LEV * B_DEV, 128), F32),
            pltpu.SemaphoreType.DMA((2, 5)),
        ],
        compiler_params=pltpu.CompilerParams(vmem_limit_bytes=VMEM_BYTES),
    )(result, crm_new)
    crm_out = jnp.transpose(crm_out.reshape(LEV, B_DEV, 128), (1, 0, 2))
    return dyn_out.reshape(dyn_field.shape), crm_out


def solution(mesh):
    placed = (P(None, "ex", "ey"), P(("ex", "ey"), None, None), P(("ex", "ey")), P(("ex", "ey")))
    return jax.shard_map(
        functools.partial(shards, (mesh.shape["ex"], mesh.shape["ey"])),
        mesh=mesh,
        in_specs=placed,
        out_specs=(P(None, "ex", "ey"), P(("ex", "ey"), None, None)),
        check_vma=False,
    )
```

```python
import functools

import jax
import jax.numpy as jnp
import numpy as np
from jax import lax
from jax.experimental import pallas as pl
from jax.experimental.pallas import tpu as pltpu
from jax.sharding import PartitionSpec as P

F32 = jnp.float32
BF16 = jnp.bfloat16
MESH = pl.DeviceIdType.MESH

GLEV, LEV, COLS, CX, CY, B_DEV, MAXSUB = 72, 58, 64, 8, 128, 32, 12
PER_ROW = B_DEV // CX
STRIDE = CY // PER_ROW
ROWS = LEV * CX
GROWS = GLEV * CX
PAD = 8
SETS = PER_ROW // 2
CUTS = (0, 16, 30, 44, 58)
HALO = 3
PACK = 16
BATCH = 8
PACKS = (GLEV + PACK - 1) // PACK
GROUPS = GLEV // 8
CHUNKS = 2
VMEM_BYTES = 60 * 1024 * 1024
RATE = 0.3 * float(np.log2(np.e))
SCALED_T = RATE
SCALED_Q = 2.0
AROUND = [(0, 1), (1, 1), (-1, 1), (0, -1), (1, -1), (-1, -1), (1, 0), (-1, 0)]


def tables(step, pick, mean):
    def iotas(shape):
        return (lax.broadcasted_iota(jnp.int32, shape, d) for d in range(2))

    def where(flag, value):
        return jnp.where(flag, value, 0.0)

    row, col = iotas((256, 256))
    gap = (row - col) & (COLS - 1)
    same = row // COLS == col // COLS
    near = same & ((gap == 0) | (gap == 1) | (gap == COLS - 1))
    block = where(near, 1.0) - where(same & (row < 128), 1.0 / 128.0)
    step[0:256, :] = block.astype(BF16)
    step[256:512, :] = block.astype(BF16)
    block = where((row & 127) == STRIDE * (col // COLS), 1.0)
    pick[...] = block.astype(BF16)
    row, col = iotas((256, 128))
    for j in range(SETS):
        block = where(col == STRIDE * (2 * j + (row & 127) // COLS), 1.0 / COLS)
        mean[256 * j : 256 * j + 256, :] = block.astype(BF16)


def split(x):
    high = x.astype(BF16)
    return high, (x - high.astype(F32)).astype(BF16)


def dot(terms, m):
    return jnp.dot(jnp.concatenate(terms, axis=1), m, preferred_element_type=F32)


def kernel(
    sizes, sub_hbm, slot_hbm, dyn_hbm, crm_hbm,
    dyn_hbm_out, crm_hbm_out,
    result, crm_new, field, crm, sub, slot, step, pick, mean, temp, moist, pull,
    tall, send_rows, recv_rows, send_cols, recv_cols, send_far, recv_far, edge,
    load_sem, in_sem, out_sem, send_sem, recv_sem, ready_sem,
):
    nex, ney = sizes
    ex, ey = lax.axis_index("ex"), lax.axis_index("ey")

    def device(dx, dy):
        return lax.rem(ex + dx + nex, nex), lax.rem(ey + dy + ney, ney)

    first = (ex == 0) & (ey == 0)
    last_ey = ey == ney - 1

    def answers(dx, dy):
        x, y = device(dx, dy)
        to_first = (x == 0) & (y == 0) & jnp.logical_not(last_ey)
        return to_first | (ey == 0) | last_ey if dy == -1 else to_first

    def awaited(dx, dy):
        if dy == 1:
            return last_ey | first | (ey == ney - 2)
        return first if dy == 0 else first & (ey > 0)

    def indirect(dx, dy):
        return last_ey if dy == 0 else ey < 0

    barrier = pltpu.get_barrier_semaphore()
    for at in AROUND:
        @pl.when(jnp.logical_not(awaited(*at) | indirect(*at)))
        def _():
            pl.semaphore_signal(barrier, inc=1, device_id=device(*at), device_id_type=MESH)

    small = [(dyn_hbm, field), (sub_hbm, sub), (slot_hbm, slot)]
    small = [pltpu.make_async_copy(src, dst, load_sem.at[i]) for i, (src, dst) in enumerate(small)]
    for copy in small:
        copy.start()
    loads = []
    per = LEV * B_DEV // CHUNKS
    for c in range(CHUNKS):
        part = pl.ds(c * per, per)
        loads.append(pltpu.make_async_copy(crm_hbm.at[part], crm.at[part], in_sem.at[c]))
        loads[-1].start()

    lane8 = lax.broadcasted_iota(jnp.int32, (8, 128), 1)
    row8 = lax.broadcasted_iota(jnp.int32, (8, 128), 0)
    left8 = lane8 < COLS
    zero = jnp.zeros((8, 128), F32)

    small[0].wait()
    for r in range(HALO):
        send_rows[1, r] = field[pl.ds(CX - 1 - r, GLEV, stride=CX), :]
    for r in range(HALO):
        send_rows[0, r] = field[pl.ds(r, GLEV, stride=CX), :]

    copies = []
    for k, (dx, dy) in enumerate(AROUND):
        side = (dy + 1) // 2
        if dy == 0:
            src, dst = send_rows.at[(dx + 1) // 2], recv_rows.at[(1 - dx) // 2]
        elif dx == 0:
            src, dst = send_cols.at[side], recv_cols.at[1 - side]
        else:
            src, dst = send_far.at[(dx + 1) // 2, side], recv_far.at[(1 - dx) // 2, 1 - side]
        copies.append(
            pltpu.make_async_remote_copy(
                src_ref=src,
                dst_ref=dst,
                send_sem=send_sem.at[k],
                recv_sem=recv_sem.at[k],
                device_id=device(dx, dy),
                device_id_type=MESH,
            )
        )

    for end in range(2):
        for r in range(2):
            head, tail = zero, zero
            for g in range(GROUPS):
                tile = send_rows[end, r, 8 * g : 8 * g + 8, :]
                tile = pltpu.roll(tile, 8 * g, 1) if g else tile
                head = jnp.where(lane8 // 8 == g, tile, head)
                tail = jnp.where(lane8 // 8 == (g - 1) % 16, tile, tail)
            send_far[end, 0, r] = head
            send_far[end, 1, r] = tail
    for g in range(PACKS):
        head, tail = zero, zero
        for i in range(min(PACK, GLEV - g * PACK)):
            tile = field[pl.ds((g * PACK + i) * CX, CX), :]
            tile = pltpu.roll(tile, 8 * i, 1) if i else tile
            head = jnp.where(lane8 // 8 == i, tile, head)
            tail = jnp.where(lane8 // 8 == (i - 1) % PACK, tile, tail)
        send_cols[0, g] = head
        send_cols[1, g] = tail

    n_answers = sum(jnp.where(answers(*at), 1, 0) for at in AROUND)
    pl.semaphore_wait(barrier, len(AROUND) - n_answers - jnp.where(last_ey, 2, 0))
    for at in AROUND:
        @pl.when(awaited(*at))
        def _():
            pl.semaphore_signal(ready_sem, inc=1, device_id=device(*at), device_id_type=MESH)
    for at, copy in zip(AROUND, copies):
        pl.when(jnp.logical_not(answers(*at) | indirect(*at)))(copy.start)

    small[1].wait()
    small[2].wait()
    active = jnp.where(slot[...] >= 0, sub[...], 0).astype(F32)
    lane32 = lax.broadcasted_iota(jnp.int32, (CX, B_DEV), 1)
    row32 = lax.broadcasted_iota(jnp.int32, (CX, B_DEV), 0)
    spread_out = jnp.broadcast_to(active, (CX, B_DEV))
    counts = []
    for k in range(PER_ROW):
        own = jnp.where(lane32 == PER_ROW * row32 + k, spread_out, 0.0)
        counts.append(jnp.sum(own, axis=1, keepdims=True))
    counts = [jnp.where(left8, counts[2 * j], counts[2 * j + 1]) for j in range(SETS)]

    for side in range(2):
        for j in range(SETS):
            for buf in (temp, moist):
                buf[side, j, 0:PAD, :] = zero
                buf[side, j, PAD + ROWS : PAD + ROWS + PAD, :] = zero

    tables(step, pick, mean)
    for a, b in zip(CUTS[:-1], CUTS[1:]):
        here = pl.ds(a * CX, (b - a) * CX)
        wide = (0.1 * SCALED_T) * dot(split(field[here, :]), pick[...])
        for j in range(SETS):
            pull[j, here, :] = wide[:, 128 * j : 128 * j + 128]

    def warm_and_moist(j, level):
        one, two = (crm[pl.ds(level * B_DEV + 2 * j + i, CX, stride=PER_ROW), :] for i in range(2))
        t = jnp.where(left8, one, pltpu.roll(two, COLS, 1))
        q = jnp.where(left8, pltpu.roll(one, COLS, 1), two)
        return t, q

    for load in loads:
        load.wait()
    for level in range(LEV):
        for j in range(SETS):
            t, q = warm_and_moist(j, level)
            temp[0, j, pl.ds(PAD + level * CX, CX), :] = SCALED_T * t
            moist[0, j, pl.ds(PAD + level * CX, CX), :] = SCALED_Q * q

    def substep(n, old, new):
        for j in range(SETS):
            on = n < counts[j]
            for a, b in zip(CUTS[:-1], CUTS[1:]):
                base, rows = PAD + a * CX, (b - a) * CX
                here, up, down = (pl.ds(base + s, rows) for s in (0, CX, -CX))
                t, q = temp[old, j, here, :], moist[old, j, here, :]
                (t1, t2), (q1, q2) = split(t), split(q)
                across = dot([t1, q1, t2, q2], step[...])
                vt = temp[old, j, up, :] + temp[old, j, down, :]
                vq = moist[old, j, up, :] + moist[old, j, down, :]
                e = jnp.maximum(q - jnp.exp2(t), 0.0)
                t_new = 0.2 * (across[:, :128] + vt) + (pull[j, pl.ds(a * CX, rows), :] + (0.125 * SCALED_T) * e)
                q_new = 0.2 * (across[:, 128:] + vq) - 0.5 * e
                mask = jnp.concatenate([on] * (b - a), axis=0)
                temp[new, j, here, :] = jnp.where(mask, t_new, t)
                moist[new, j, here, :] = jnp.where(mask, q_new, q)

    @pl.loop(0, MAXSUB // 2)
    def _(n):
        now = (2 * n).astype(F32)
        substep(now, 0, 1)
        substep(now + 1.0, 1, 0)

    outs = []
    for c in range(CHUNKS):
        for level in range(c * LEV // CHUNKS, (c + 1) * LEV // CHUNKS):
            for j in range(SETS):
                own = pl.ds(PAD + level * CX, CX)
                t = (1.0 / SCALED_T) * temp[0, j, own, :]
                q = (1.0 / SCALED_Q) * moist[0, j, own, :]
                temp[1, j, own, :] = t - warm_and_moist(j, level)[0]
                at = [pl.ds(level * B_DEV + 2 * j + i, CX, stride=PER_ROW) for i in range(2)]
                crm_new[at[0], :] = jnp.where(left8, t, pltpu.roll(q, COLS, 1))
                crm_new[at[1], :] = jnp.where(left8, pltpu.roll(t, COLS, 1), q)
        part = pl.ds(c * per, per)
        outs.append(pltpu.make_async_copy(crm_new.at[part], crm_hbm_out.at[part], out_sem.at[c]))
        outs[-1].start()

    def spread(c, e):
        lane = lax.broadcasted_iota(jnp.int32, c.shape, 1)
        first_lane, last_lane = lane == 0, lane == CY - 1
        cr, cl = pltpu.roll(c, 1, 1), pltpu.roll(c, CY - 1, 1)
        er, el = pltpu.roll(e, 1, 1), pltpu.roll(e, CY - 1, 1)
        c_new = c + (jnp.where(first_lane, er, cr) + jnp.where(last_lane, el, cl))
        e_new = e + (jnp.where(first_lane, cr, er) + jnp.where(last_lane, cl, el))
        return c_new, e_new

    for level in range(GLEV):
        tall[pl.ds(level * 24, 8), :] = zero
        tall[pl.ds(level * 24 + 8, CX), :] = field[pl.ds(level * CX, CX), :]
        tall[pl.ds(level * 24 + 16, 8), :] = zero
    for start in range(0, GLEV, BATCH):
        at = [
            jnp.concatenate([tall[pl.ds((start + i) * 24 + 8 + k, 8), :] for i in range(BATCH)])
            for k in range(-HALO, HALO + 1)
        ]
        c0, c1, c2, c3 = at[3], at[2] + at[4], at[1] + at[5], at[0] + at[6]
        x, y = spread(c0, jnp.zeros_like(c0))
        x, y = spread(x + 3.0 * c1, y)
        x, y = spread(x + (6.0 * c0 + 3.0 * c2), y)
        result[pl.ds(start * CX, BATCH * CX), :] = 0.008 * (x + (3.0 * c1 + c3))
    for a, b in zip(CUTS[:-1], CUTS[1:]):
        here, padded = pl.ds(a * CX, (b - a) * CX), pl.ds(PAD + a * CX, (b - a) * CX)
        change = [part for j in range(SETS) for part in split(temp[1, j, padded, :])]
        result[here, :] += dot(change, mean[...])

    def take(k):
        if k == from_across:
            pl.when(jnp.logical_not(last_ey))(copies[k].wait_recv)
        else:
            copies[k].wait_recv()

    def add_rows(end, h1, h2, h3, e1, e2):
        u, v = spread(h1, e1)
        w, _ = spread(u + h2, v + e2)
        for r, add in enumerate((3.0 * (w + h1) + h3, 3.0 * u + h2, h1)):
            result[pl.ds(CX - 1 - r if end else r, GLEV, stride=CX), :] += 0.008 * add

    @pl.when(n_answers > 0)
    def _():
        pl.semaphore_wait(ready_sem, n_answers)

    for at, copy in zip(AROUND, copies):
        pl.when(answers(*at))(copy.start)
    from_across = AROUND.index((0, -1))

    @pl.when(last_ey)
    def _():
        copies[from_across].wait_recv()
        for at, copy in zip(AROUND, copies):
            if at[1] == 0:
                copy.start()

    nothing = jnp.zeros((GLEV, CY), F32)
    for dx in (-1, 1):
        take(AROUND.index((dx, 0)))
        end = (1 - dx) // 2
        add_rows(end, *(recv_rows[end, r] for r in range(HALO)), nothing, nothing)

    tiles = 2 * PACKS
    for i in range(tiles):
        edge[24 * i : 24 * i + 8, :] = zero
        edge[24 * i + 16 : 24 * i + 24, :] = zero
    slot8 = lane8 % 8
    low_lanes = slot8 < 4

    for dy in (-1, 1):
        for k, at in enumerate(AROUND):
            if at[1] == dy:
                take(k)
    for i in range(tiles):
        side, g = i // PACKS, i % PACKS
        beyond = (slot8 >= 5) if side == 0 else (slot8 < 3)
        edge[24 * i + 8 : 24 * i + 16, :] = jnp.where(beyond, recv_cols[side, g], 0.0)
    at = [
        jnp.concatenate([edge[pl.ds(24 * i + 8 + k, 8), :] for i in range(tiles)]) for k in range(-HALO, HALO + 1)
    ]
    c0, c1, c2, c3 = at[3], at[2] + at[4], at[1] + at[5], at[0] + at[6]
    slots = lax.broadcasted_iota(jnp.int32, c0.shape, 1) % 8
    valid = (slots >= 5) | (slots < 3)

    def near(x):
        return x + jnp.where(valid, pltpu.roll(x, 1, 1) + pltpu.roll(x, CY - 1, 1), 0.0)

    far = [jnp.where(low_lanes, recv_far[end, 1, r], recv_far[end, 0, r]) for r in range(2) for end in range(2)]
    far = [
        jnp.concatenate([pltpu.roll(x, 128 - 8 * g, 1) if g else x for x in far[2 * r : 2 * r + 2] for g in range(GROUPS)])
        for r in range(2)
    ]
    u, v = spread(jnp.zeros_like(far[0]), far[0])
    x = near(c0)
    w, _ = spread(u, v + far[1])
    x = near(x + 3.0 * c1)
    x = 0.008 * near(x + (6.0 * c0 + 3.0 * c2))
    for end in range(2):
        part = slice(end * GLEV, end * GLEV + GLEV)
        for r, add in enumerate((3.0 * w[part], 3.0 * u[part])):
            result[pl.ds(CX - 1 - r if end else r, GLEV, stride=CX), :] += 0.008 * add
    for g in range(PACKS):
        both = jnp.where(low_lanes, x[8 * g : 8 * g + 8], x[8 * (g + PACKS) : 8 * (g + PACKS) + 8])
        levels = range(g * PACK, min(GLEV, g * PACK + PACK))
        add = jnp.concatenate([pltpu.roll(both, 128 - 8 * (i % PACK), 1) if i % PACK else both for i in levels])
        lane = lax.broadcasted_iota(jnp.int32, add.shape, 1)
        own = pl.ds(levels[0] * CX, len(levels) * CX)
        result[own, :] += jnp.where((lane < 3) | (lane >= CY - 3), add, 0.0)
    outs.append(pltpu.make_async_copy(result, dyn_hbm_out, out_sem.at[CHUNKS]))
    outs[-1].start()
    for copy in copies:
        copy.wait_send()
    for out in outs:
        out.wait()


def write(result, crm_new, dyn_out, crm_out, result_held, crm_held, sems):
    ins, outs = [], []
    for src, held, dst, n in ((result, result_held, dyn_out, 1), (crm_new, crm_held, crm_out, 4)):
        rows = src.shape[0] // n
        for c in range(n):
            part = pl.ds(c * rows, rows)
            ins.append(pltpu.make_async_copy(src.at[part], held.at[part], sems.at[0, len(ins)]))
            outs.append(pltpu.make_async_copy(held.at[part], dst.at[part], sems.at[1, len(outs)]))
    for load in ins:
        load.start()
    for load, store in zip(ins, outs):
        load.wait()
        store.start()
    for store in outs:
        store.wait()


def shards(sizes, dyn_field, crm_state, subcycles, dest_slot):
    hbm = pl.BlockSpec(memory_space=pltpu.HBM)
    state = (2, SETS, ROWS + 2 * PAD, 128)
    dyn_shape = jax.ShapeDtypeStruct((GROWS, CY), F32)
    crm_shape = jax.ShapeDtypeStruct((LEV * B_DEV, 128), F32)
    result, crm_new = pl.pallas_call(
        functools.partial(kernel, sizes),
        out_shape=(dyn_shape, crm_shape),
        in_specs=[hbm] * 4,
        out_specs=(hbm, hbm),
        scratch_shapes=[
            pltpu.VMEM((GROWS, CY), F32),
            pltpu.VMEM((LEV * B_DEV, 128), F32),
            pltpu.VMEM((GROWS, CY), F32),
            pltpu.VMEM((LEV * B_DEV, 128), F32),
            pltpu.VMEM((1, B_DEV), jnp.int32),
            pltpu.VMEM((1, B_DEV), jnp.int32),
            pltpu.VMEM((512, 256), BF16),
            pltpu.VMEM((256, 256), BF16),
            pltpu.VMEM((512, 128), BF16),
            pltpu.VMEM(state, F32),
            pltpu.VMEM(state, F32),
            pltpu.VMEM((SETS, ROWS, 128), F32),
            pltpu.VMEM((GLEV * 24, CY), F32),
            pltpu.VMEM((2, HALO, GLEV, CY), F32),
            pltpu.VMEM((2, HALO, GLEV, CY), F32),
            pltpu.VMEM((2, PACKS, 8, 128), F32),
            pltpu.VMEM((2, PACKS, 8, 128), F32),
            pltpu.VMEM((2, 2, 2, 8, 128), F32),
            pltpu.VMEM((2, 2, 2, 8, 128), F32),
            pltpu.VMEM((2 * PACKS * 24, 128), F32),
            pltpu.SemaphoreType.DMA((3,)),
            pltpu.SemaphoreType.DMA((CHUNKS,)),
            pltpu.SemaphoreType.DMA((CHUNKS + 1,)),
            pltpu.SemaphoreType.DMA((8,)),
            pltpu.SemaphoreType.DMA((8,)),
            pltpu.SemaphoreType.REGULAR,
        ],
        compiler_params=pltpu.CompilerParams(
            collective_id=0, has_side_effects=True, vmem_limit_bytes=VMEM_BYTES
        ),
    )(
        subcycles.reshape(1, B_DEV),
        dest_slot.reshape(1, B_DEV),
        dyn_field.reshape(GROWS, CY),
        jnp.transpose(crm_state, (1, 0, 2)).reshape(LEV * B_DEV, 128),
    )
    dyn_out, crm_out = pl.pallas_call(
        write,
        out_shape=(dyn_shape, crm_shape),
        in_specs=[hbm] * 2,
        out_specs=(hbm, hbm),
        scratch_shapes=[
            pltpu.VMEM((GROWS, CY), F32),
            pltpu.VMEM((LEV * B_DEV, 128), F32),
            pltpu.SemaphoreType.DMA((2, 5)),
        ],
        compiler_params=pltpu.CompilerParams(vmem_limit_bytes=VMEM_BYTES),
    )(result, crm_new)
    crm_out = jnp.transpose(crm_out.reshape(LEV, B_DEV, 128), (1, 0, 2))
    return dyn_out.reshape(dyn_field.shape), crm_out


def solution(mesh):
    placed = (P(None, "ex", "ey"), P(("ex", "ey"), None, None), P(("ex", "ey")), P(("ex", "ey")))
    return jax.shard_map(
        functools.partial(shards, (mesh.shape["ex"], mesh.shape["ey"])),
        mesh=mesh,
        in_specs=placed,
        out_specs=(P(None, "ex", "ey"), P(("ex", "ey"), None, None)),
        check_vma=False,
    )
```

```python
import functools

import jax
import jax.numpy as jnp
import numpy as np
from jax import lax
from jax.experimental import pallas as pl
from jax.experimental.pallas import tpu as pltpu
from jax.sharding import PartitionSpec as P

F32 = jnp.float32
BF16 = jnp.bfloat16
MESH = pl.DeviceIdType.MESH

GLEV, LEV, COLS, CX, CY, B_DEV, MAXSUB = 72, 58, 64, 8, 128, 32, 12
PER_ROW = B_DEV // CX
STRIDE = CY // PER_ROW
ROWS = LEV * CX
GROWS = GLEV * CX
PAD = 8
SETS = PER_ROW // 2
CUTS = (0, 16, 30, 44, 58)
HALO = 3
PACK = 16
BATCH = 8
PACKS = (GLEV + PACK - 1) // PACK
GROUPS = GLEV // 8
CHUNKS = 2
VMEM_BYTES = 60 * 1024 * 1024
RATE = 0.3 * float(np.log2(np.e))
SCALED_T = RATE
SCALED_Q = 2.0
AROUND = [(0, 1), (1, 1), (-1, 1), (0, -1), (1, -1), (-1, -1), (1, 0), (-1, 0)]


def tables(step, pick, mean):
    def iotas(shape):
        return (lax.broadcasted_iota(jnp.int32, shape, d) for d in range(2))

    def where(flag, value):
        return jnp.where(flag, value, 0.0)

    row, col = iotas((256, 256))
    gap = (row - col) & (COLS - 1)
    same = row // COLS == col // COLS
    near = same & ((gap == 0) | (gap == 1) | (gap == COLS - 1))
    block = where(near, 1.0) - where(same & (row < 128), 1.0 / 128.0)
    step[0:256, :] = block.astype(BF16)
    step[256:512, :] = block.astype(BF16)
    block = where((row & 127) == STRIDE * (col // COLS), 1.0)
    pick[...] = block.astype(BF16)
    row, col = iotas((256, 128))
    for j in range(SETS):
        block = where(col == STRIDE * (2 * j + (row & 127) // COLS), 1.0 / COLS)
        mean[256 * j : 256 * j + 256, :] = block.astype(BF16)


def split(x):
    high = x.astype(BF16)
    return high, (x - high.astype(F32)).astype(BF16)


def dot(terms, m):
    return jnp.dot(jnp.concatenate(terms, axis=1), m, preferred_element_type=F32)


def kernel(
    sizes, sub_hbm, slot_hbm, dyn_hbm, crm_hbm,
    dyn_hbm_out, crm_hbm_out,
    result, crm_new, field, crm, sub, slot, step, pick, mean, temp, moist, pull,
    tall, send_rows, recv_rows, send_cols, recv_cols, send_far, recv_far, edge,
    load_sem, in_sem, out_sem, send_sem, recv_sem, ready_sem,
):
    nex, ney = sizes
    ex, ey = lax.axis_index("ex"), lax.axis_index("ey")

    def device(dx, dy):
        return lax.rem(ex + dx + nex, nex), lax.rem(ey + dy + ney, ney)

    first = (ex == 0) & (ey == 0)
    last_ey = ey == ney - 1

    def answers(dx, dy):
        x, y = device(dx, dy)
        to_first = (x == 0) & (y == 0) & jnp.logical_not(last_ey)
        return to_first | (ey == 0) | last_ey if dy == -1 else to_first

    def awaited(dx, dy):
        if dy == 1:
            return last_ey | first | (ey == ney - 2)
        return first if dy == 0 else first & (ey > 0)

    def indirect(dx, dy):
        return last_ey if dy == 0 else ey < 0

    barrier = pltpu.get_barrier_semaphore()
    for at in AROUND:
        @pl.when(jnp.logical_not(awaited(*at) | indirect(*at)))
        def _():
            pl.semaphore_signal(barrier, inc=1, device_id=device(*at), device_id_type=MESH)

    small = [(dyn_hbm, field), (sub_hbm, sub), (slot_hbm, slot)]
    small = [pltpu.make_async_copy(src, dst, load_sem.at[i]) for i, (src, dst) in enumerate(small)]
    for copy in small:
        copy.start()
    loads = []
    per = LEV * B_DEV // CHUNKS
    for c in range(CHUNKS):
        part = pl.ds(c * per, per)
        loads.append(pltpu.make_async_copy(crm_hbm.at[part], crm.at[part], in_sem.at[c]))
        loads[-1].start()

    lane8 = lax.broadcasted_iota(jnp.int32, (8, 128), 1)
    row8 = lax.broadcasted_iota(jnp.int32, (8, 128), 0)
    left8 = lane8 < COLS
    zero = jnp.zeros((8, 128), F32)

    small[0].wait()
    for r in range(HALO):
        send_rows[1, r] = field[pl.ds(CX - 1 - r, GLEV, stride=CX), :]
    for r in range(HALO):
        send_rows[0, r] = field[pl.ds(r, GLEV, stride=CX), :]

    copies = []
    for k, (dx, dy) in enumerate(AROUND):
        side = (dy + 1) // 2
        if dy == 0:
            src, dst = send_rows.at[(dx + 1) // 2], recv_rows.at[(1 - dx) // 2]
        elif dx == 0:
            src, dst = send_cols.at[side], recv_cols.at[1 - side]
        else:
            src, dst = send_far.at[(dx + 1) // 2, side], recv_far.at[(1 - dx) // 2, 1 - side]
        copies.append(
            pltpu.make_async_remote_copy(
                src_ref=src,
                dst_ref=dst,
                send_sem=send_sem.at[k],
                recv_sem=recv_sem.at[k],
                device_id=device(dx, dy),
                device_id_type=MESH,
            )
        )

    for end in range(2):
        for r in range(2):
            head, tail = zero, zero
            for g in range(GROUPS):
                tile = send_rows[end, r, 8 * g : 8 * g + 8, :]
                tile = pltpu.roll(tile, 8 * g, 1) if g else tile
                head = jnp.where(lane8 // 8 == g, tile, head)
                tail = jnp.where(lane8 // 8 == (g - 1) % 16, tile, tail)
            send_far[end, 0, r] = head
            send_far[end, 1, r] = tail
    for g in range(PACKS):
        head, tail = zero, zero
        for i in range(min(PACK, GLEV - g * PACK)):
            tile = field[pl.ds((g * PACK + i) * CX, CX), :]
            tile = pltpu.roll(tile, 8 * i, 1) if i else tile
            head = jnp.where(lane8 // 8 == i, tile, head)
            tail = jnp.where(lane8 // 8 == (i - 1) % PACK, tile, tail)
        send_cols[0, g] = head
        send_cols[1, g] = tail

    n_answers = sum(jnp.where(answers(*at), 1, 0) for at in AROUND)
    pl.semaphore_wait(barrier, len(AROUND) - n_answers - jnp.where(last_ey, 2, 0))
    for at in AROUND:
        @pl.when(awaited(*at))
        def _():
            pl.semaphore_signal(ready_sem, inc=1, device_id=device(*at), device_id_type=MESH)
    for at, copy in zip(AROUND, copies):
        pl.when(jnp.logical_not(answers(*at) | indirect(*at)))(copy.start)

    small[1].wait()
    small[2].wait()
    active = jnp.where(slot[...] >= 0, sub[...], 0).astype(F32)
    lane32 = lax.broadcasted_iota(jnp.int32, (CX, B_DEV), 1)
    row32 = lax.broadcasted_iota(jnp.int32, (CX, B_DEV), 0)
    spread_out = jnp.broadcast_to(active, (CX, B_DEV))
    counts = []
    for k in range(PER_ROW):
        own = jnp.where(lane32 == PER_ROW * row32 + k, spread_out, 0.0)
        counts.append(jnp.sum(own, axis=1, keepdims=True))
    counts = [jnp.where(left8, counts[2 * j], counts[2 * j + 1]) for j in range(SETS)]

    for side in range(2):
        for j in range(SETS):
            for buf in (temp, moist):
                buf[side, j, 0:PAD, :] = zero
                buf[side, j, PAD + ROWS : PAD + ROWS + PAD, :] = zero

    tables(step, pick, mean)
    for a, b in zip(CUTS[:-1], CUTS[1:]):
        here = pl.ds(a * CX, (b - a) * CX)
        wide = (0.1 * SCALED_T) * dot(split(field[here, :]), pick[...])
        for j in range(SETS):
            pull[j, here, :] = wide[:, 128 * j : 128 * j + 128]

    def warm_and_moist(j, level):
        one, two = (crm[pl.ds(level * B_DEV + 2 * j + i, CX, stride=PER_ROW), :] for i in range(2))
        t = jnp.where(left8, one, pltpu.roll(two, COLS, 1))
        q = jnp.where(left8, pltpu.roll(one, COLS, 1), two)
        return t, q

    for load in loads:
        load.wait()
    for level in range(LEV):
        for j in range(SETS):
            t, q = warm_and_moist(j, level)
            temp[0, j, pl.ds(PAD + level * CX, CX), :] = SCALED_T * t
            moist[0, j, pl.ds(PAD + level * CX, CX), :] = SCALED_Q * q

    def substep(n, old, new):
        for j in range(SETS):
            on = n < counts[j]
            for a, b in zip(CUTS[:-1], CUTS[1:]):
                base, rows = PAD + a * CX, (b - a) * CX
                here, up, down = (pl.ds(base + s, rows) for s in (0, CX, -CX))
                t, q = temp[old, j, here, :], moist[old, j, here, :]
                (t1, t2), (q1, q2) = split(t), split(q)
                across = dot([t1, q1, t2, q2], step[...])
                vt = temp[old, j, up, :] + temp[old, j, down, :]
                vq = moist[old, j, up, :] + moist[old, j, down, :]
                e = jnp.maximum(q - jnp.exp2(t), 0.0)
                t_new = 0.2 * (across[:, :128] + vt) + (pull[j, pl.ds(a * CX, rows), :] + (0.125 * SCALED_T) * e)
                q_new = 0.2 * (across[:, 128:] + vq) - 0.5 * e
                mask = jnp.concatenate([on] * (b - a), axis=0)
                temp[new, j, here, :] = jnp.where(mask, t_new, t)
                moist[new, j, here, :] = jnp.where(mask, q_new, q)

    @pl.loop(0, MAXSUB // 2)
    def _(n):
        now = (2 * n).astype(F32)
        substep(now, 0, 1)
        substep(now + 1.0, 1, 0)

    outs = []
    for c in range(CHUNKS):
        for level in range(c * LEV // CHUNKS, (c + 1) * LEV // CHUNKS):
            for j in range(SETS):
                own = pl.ds(PAD + level * CX, CX)
                t = (1.0 / SCALED_T) * temp[0, j, own, :]
                q = (1.0 / SCALED_Q) * moist[0, j, own, :]
                temp[1, j, own, :] = t - warm_and_moist(j, level)[0]
                at = [pl.ds(level * B_DEV + 2 * j + i, CX, stride=PER_ROW) for i in range(2)]
                crm_new[at[0], :] = jnp.where(left8, t, pltpu.roll(q, COLS, 1))
                crm_new[at[1], :] = jnp.where(left8, pltpu.roll(t, COLS, 1), q)
        part = pl.ds(c * per, per)
        outs.append(pltpu.make_async_copy(crm_new.at[part], crm_hbm_out.at[part], out_sem.at[c]))
        outs[-1].start()

    def spread(c, e):
        lane = lax.broadcasted_iota(jnp.int32, c.shape, 1)
        first_lane, last_lane = lane == 0, lane == CY - 1
        cr, cl = pltpu.roll(c, 1, 1), pltpu.roll(c, CY - 1, 1)
        er, el = pltpu.roll(e, 1, 1), pltpu.roll(e, CY - 1, 1)
        c_new = c + (jnp.where(first_lane, er, cr) + jnp.where(last_lane, el, cl))
        e_new = e + (jnp.where(first_lane, cr, er) + jnp.where(last_lane, cl, el))
        return c_new, e_new

    for level in range(GLEV):
        tall[pl.ds(level * 24, 8), :] = zero
        tall[pl.ds(level * 24 + 8, CX), :] = field[pl.ds(level * CX, CX), :]
        tall[pl.ds(level * 24 + 16, 8), :] = zero
    for start in range(0, GLEV, BATCH):
        at = [
            jnp.concatenate([tall[pl.ds((start + i) * 24 + 8 + k, 8), :] for i in range(BATCH)])
            for k in range(-HALO, HALO + 1)
        ]
        c0, c1, c2, c3 = at[3], at[2] + at[4], at[1] + at[5], at[0] + at[6]
        x, y = spread(c0, jnp.zeros_like(c0))
        x, y = spread(x + 3.0 * c1, y)
        x, y = spread(x + (6.0 * c0 + 3.0 * c2), y)
        result[pl.ds(start * CX, BATCH * CX), :] = 0.008 * (x + (3.0 * c1 + c3))
    for a, b in zip(CUTS[:-1], CUTS[1:]):
        here, padded = pl.ds(a * CX, (b - a) * CX), pl.ds(PAD + a * CX, (b - a) * CX)
        change = [part for j in range(SETS) for part in split(temp[1, j, padded, :])]
        result[here, :] += dot(change, mean[...])

    def take(k):
        if k == from_across:
            pl.when(jnp.logical_not(last_ey))(copies[k].wait_recv)
        else:
            copies[k].wait_recv()

    def add_rows(end, h1, h2, h3, e1, e2):
        u, v = spread(h1, e1)
        w, _ = spread(u + h2, v + e2)
        for r, add in enumerate((3.0 * (w + h1) + h3, 3.0 * u + h2, h1)):
            result[pl.ds(CX - 1 - r if end else r, GLEV, stride=CX), :] += 0.008 * add

    @pl.when(n_answers > 0)
    def _():
        pl.semaphore_wait(ready_sem, n_answers)

    for at, copy in zip(AROUND, copies):
        pl.when(answers(*at))(copy.start)
    from_across = AROUND.index((0, -1))

    @pl.when(last_ey)
    def _():
        copies[from_across].wait_recv()
        for at, copy in zip(AROUND, copies):
            if at[1] == 0:
                copy.start()

    nothing = jnp.zeros((GLEV, CY), F32)
    for dx in (-1, 1):
        take(AROUND.index((dx, 0)))
        end = (1 - dx) // 2
        add_rows(end, *(recv_rows[end, r] for r in range(HALO)), nothing, nothing)

    tiles = 2 * PACKS
    for i in range(tiles):
        edge[24 * i : 24 * i + 8, :] = zero
        edge[24 * i + 16 : 24 * i + 24, :] = zero
    slot8 = lane8 % 8
    low_lanes = slot8 < 4

    for dy in (-1, 1):
        for k, at in enumerate(AROUND):
            if at[1] == dy:
                take(k)
    for i in range(tiles):
        side, g = i // PACKS, i % PACKS
        beyond = (slot8 >= 5) if side == 0 else (slot8 < 3)
        edge[24 * i + 8 : 24 * i + 16, :] = jnp.where(beyond, recv_cols[side, g], 0.0)
    at = [
        jnp.concatenate([edge[pl.ds(24 * i + 8 + k, 8), :] for i in range(tiles)]) for k in range(-HALO, HALO + 1)
    ]
    c0, c1, c2, c3 = at[3], at[2] + at[4], at[1] + at[5], at[0] + at[6]
    slots = lax.broadcasted_iota(jnp.int32, c0.shape, 1) % 8
    valid = (slots >= 5) | (slots < 3)

    def near(x):
        return x + jnp.where(valid, pltpu.roll(x, 1, 1) + pltpu.roll(x, CY - 1, 1), 0.0)

    far = [jnp.where(low_lanes, recv_far[end, 1, r], recv_far[end, 0, r]) for r in range(2) for end in range(2)]
    far = [
        jnp.concatenate([pltpu.roll(x, 128 - 8 * g, 1) if g else x for x in far[2 * r : 2 * r + 2] for g in range(GROUPS)])
        for r in range(2)
    ]
    u, v = spread(jnp.zeros_like(far[0]), far[0])
    x = near(c0)
    w, _ = spread(u, v + far[1])
    x = near(x + 3.0 * c1)
    x = 0.008 * near(x + (6.0 * c0 + 3.0 * c2))
    for end in range(2):
        part = slice(end * GLEV, end * GLEV + GLEV)
        for r, add in enumerate((3.0 * w[part], 3.0 * u[part])):
            result[pl.ds(CX - 1 - r if end else r, GLEV, stride=CX), :] += 0.008 * add
    for g in range(PACKS):
        both = jnp.where(low_lanes, x[8 * g : 8 * g + 8], x[8 * (g + PACKS) : 8 * (g + PACKS) + 8])
        levels = range(g * PACK, min(GLEV, g * PACK + PACK))
        add = jnp.concatenate([pltpu.roll(both, 128 - 8 * (i % PACK), 1) if i % PACK else both for i in levels])
        lane = lax.broadcasted_iota(jnp.int32, add.shape, 1)
        own = pl.ds(levels[0] * CX, len(levels) * CX)
        result[own, :] += jnp.where((lane < 3) | (lane >= CY - 3), add, 0.0)
        outs.append(pltpu.make_async_copy(result.at[own], dyn_hbm_out.at[own], out_sem.at[CHUNKS + g]))
        outs[-1].start()
    for copy in copies:
        copy.wait_send()
    for out in outs:
        out.wait()


def write(result, crm_new, dyn_out, crm_out, result_held, crm_held, sems):
    ins, outs = [], []
    for src, held, dst, n in ((result, result_held, dyn_out, 1), (crm_new, crm_held, crm_out, 4)):
        rows = src.shape[0] // n
        for c in range(n):
            part = pl.ds(c * rows, rows)
            ins.append(pltpu.make_async_copy(src.at[part], held.at[part], sems.at[0, len(ins)]))
            outs.append(pltpu.make_async_copy(held.at[part], dst.at[part], sems.at[1, len(outs)]))
    for load in ins:
        load.start()
    for load, store in zip(ins, outs):
        load.wait()
        store.start()
    for store in outs:
        store.wait()


def shards(sizes, dyn_field, crm_state, subcycles, dest_slot):
    hbm = pl.BlockSpec(memory_space=pltpu.HBM)
    state = (2, SETS, ROWS + 2 * PAD, 128)
    dyn_shape = jax.ShapeDtypeStruct((GROWS, CY), F32)
    crm_shape = jax.ShapeDtypeStruct((LEV * B_DEV, 128), F32)
    result, crm_new = pl.pallas_call(
        functools.partial(kernel, sizes),
        out_shape=(dyn_shape, crm_shape),
        in_specs=[hbm] * 4,
        out_specs=(hbm, hbm),
        scratch_shapes=[
            pltpu.VMEM((GROWS, CY), F32),
            pltpu.VMEM((LEV * B_DEV, 128), F32),
            pltpu.VMEM((GROWS, CY), F32),
            pltpu.VMEM((LEV * B_DEV, 128), F32),
            pltpu.VMEM((1, B_DEV), jnp.int32),
            pltpu.VMEM((1, B_DEV), jnp.int32),
            pltpu.VMEM((512, 256), BF16),
            pltpu.VMEM((256, 256), BF16),
            pltpu.VMEM((512, 128), BF16),
            pltpu.VMEM(state, F32),
            pltpu.VMEM(state, F32),
            pltpu.VMEM((SETS, ROWS, 128), F32),
            pltpu.VMEM((GLEV * 24, CY), F32),
            pltpu.VMEM((2, HALO, GLEV, CY), F32),
            pltpu.VMEM((2, HALO, GLEV, CY), F32),
            pltpu.VMEM((2, PACKS, 8, 128), F32),
            pltpu.VMEM((2, PACKS, 8, 128), F32),
            pltpu.VMEM((2, 2, 2, 8, 128), F32),
            pltpu.VMEM((2, 2, 2, 8, 128), F32),
            pltpu.VMEM((2 * PACKS * 24, 128), F32),
            pltpu.SemaphoreType.DMA((3,)),
            pltpu.SemaphoreType.DMA((CHUNKS,)),
            pltpu.SemaphoreType.DMA((CHUNKS + PACKS,)),
            pltpu.SemaphoreType.DMA((8,)),
            pltpu.SemaphoreType.DMA((8,)),
            pltpu.SemaphoreType.REGULAR,
        ],
        compiler_params=pltpu.CompilerParams(
            collective_id=0, has_side_effects=True, vmem_limit_bytes=VMEM_BYTES
        ),
    )(
        subcycles.reshape(1, B_DEV),
        dest_slot.reshape(1, B_DEV),
        dyn_field.reshape(GROWS, CY),
        jnp.transpose(crm_state, (1, 0, 2)).reshape(LEV * B_DEV, 128),
    )
    dyn_out, crm_out = pl.pallas_call(
        write,
        out_shape=(dyn_shape, crm_shape),
        in_specs=[hbm] * 2,
        out_specs=(hbm, hbm),
        scratch_shapes=[
            pltpu.VMEM((GROWS, CY), F32),
            pltpu.VMEM((LEV * B_DEV, 128), F32),
            pltpu.SemaphoreType.DMA((2, 5)),
        ],
        compiler_params=pltpu.CompilerParams(vmem_limit_bytes=VMEM_BYTES),
    )(result, crm_new)
    crm_out = jnp.transpose(crm_out.reshape(LEV, B_DEV, 128), (1, 0, 2))
    return dyn_out.reshape(dyn_field.shape), crm_out


def solution(mesh):
    placed = (P(None, "ex", "ey"), P(("ex", "ey"), None, None), P(("ex", "ey")), P(("ex", "ey")))
    return jax.shard_map(
        functools.partial(shards, (mesh.shape["ex"], mesh.shape["ey"])),
        mesh=mesh,
        in_specs=placed,
        out_specs=(P(None, "ex", "ey"), P(("ex", "ey"), None, None)),
        check_vma=False,
    )
```
